32 devices in a mesh: wave: 8 (over y, x, core), lev: 4 (over z).
Axes of the slice: x: 2, y: 2, z: 4, core: 2. Of those that a mesh axis runs over, the one named last changes fastest.
Arguments:
- grid_fields: float32 [8, 3, 4096, 512], P(None, None, ('wave', 'lev')), may hold values from -6 to 6
- diffusivity: bfloat16 [7, 4096, 512], P(None, ('wave', 'lev')), may hold values from 0.049804688 to 20
- tile_map: int32 [4096], replicated, may hold values from -1 to 7039, as said below
- pair_order: int32 [640], replicated, may hold values from 0 to 639, as said below
- m_order: int32 [320], replicated, may hold values from 0 to 319, each once
- legendre: bfloat16 [320, 641, 640], P('wave'), may hold values from -0.25 to 0.25
Outputs:
- spectral: float32 [320, 2, 3, 8, 641], P('wave', None, None, 'lev')
- fourier_out: bfloat16 [640, 2, 2, 3, 8, 640], P('wave', None, None, None, 'lev')
The draws below stay inside these ranges and needn't reach their ends.
Inputs may be any that keep to these rules, and one draw needn't show every extreme that they name: `tile_map`: slot s of device d (the linear index over wave and lev, wave first) is entry d * 128 + s; it holds a tile of a pair owned by wave device s // 16, or -1. Each tile p * 11 + b with b * 256 < 4 p + 20 stands in exactly one slot; no other tile appears. A permutation. Wave device w owns pair_order[w * 80 + j] for j < 80, and that pair lies in j * 8 to (j + 1) * 8 - 1. Wave device w owns the wavenumber pairs m_order[w * 40 + j], each q standing for waves q and 639 - q.
All inputs are finite; a program needn't handle non-finite values.
Results may differ from the reference program's by a relative error of at most 0.0073.
Values may be sent and summed in bfloat16 or wider, within the bound.
No kernel may reach another device: no remote copies, remote signals or barrier semaphores. Data moves between devices by JAX's collectives and lax.ppermute only.
A program may use at most 384 MiB of HBM per device.

```python
import math
import jax
import jax.numpy as jnp
from jax import lax

NPAIR = 640
NM = 640
TILE = 256
FIELDS = 3
LEV = 8
PD = 80
NMP = 320
NCOEF = 641
BLK = 11
CAPT = 16
SLOT_DEV = 128
SLOTS = 4096


def pairs_owned(key):
    wave_count = NPAIR // PD
    round_keys = jax.random.split(jax.random.fold_in(key, 11), PD)
    shuffles = jax.vmap(lambda round_key: jax.random.permutation(round_key, wave_count))(round_keys)
    ordering = jnp.arange(PD, dtype=jnp.int32)[:, None] * wave_count + shuffles.astype(jnp.int32)
    return jnp.transpose(ordering).reshape(-1).astype(jnp.int32)


def draw_pair_order(key, part):
    return pairs_owned(key)


def draw_tile_map(key, part):
    ordering = pairs_owned(key)
    wave_count = NPAIR // PD
    devices_all = SLOTS // SLOT_DEV
    slot_room = devices_all * CAPT
    length = min(PD * BLK, slot_room)
    owned = ordering.reshape(wave_count, PD)

    def one_owner(owner_pairs, owner_key):
        blocks = jnp.arange(BLK, dtype=jnp.int32)
        tile_ids = (owner_pairs[:, None] * BLK + blocks[None, :]).reshape(-1)
        usable = (blocks[None, :] * TILE < owner_pairs[:, None] * 4 + 20).reshape(-1)
        ranking = jax.random.permutation(jax.random.fold_in(owner_key, 1), PD * BLK).astype(jnp.int32)
        scores = jnp.where(usable, ranking, ranking + PD * BLK)
        sorting = jnp.argsort(scores, stable=True)
        chosen = sorting[:length]
        values = jnp.where(usable[chosen], tile_ids[chosen], -1).astype(jnp.int32)
        placing = jax.random.permutation(jax.random.fold_in(owner_key, 2), slot_room)[:length]
        return jnp.full((slot_room,), -1, jnp.int32).at[placing].set(values)
    owner_keys = jax.random.split(jax.random.fold_in(key, 12), wave_count)
    filled = jax.vmap(one_owner)(owned, owner_keys)
    filled = filled.reshape(wave_count, devices_all, CAPT)
    return jnp.transpose(filled, (1, 0, 2)).reshape(-1)


def block_scale(own_key, extent, pieces, low, top_value):
    def one(position, blocks):
        heights = jax.random.uniform(jax.random.fold_in(jax.random.fold_in(own_key, 6), position), (blocks,), jnp.float32, low / len(pieces), top_value / len(pieces))
        return jnp.repeat(jnp.exp(heights), extent[position] // blocks).reshape((-1,) + (1,) * (len(extent) - position - 1))

    level = one(*pieces[0])
    for cut in pieces[1:]:
        level = level * one(*cut)
    return level


def noise(stream_key, dims, deviation, limit, cuts=(), held_as=jnp.bfloat16):
    entries = deviation * jax.random.normal(stream_key, dims, jnp.float32)
    if cuts:
        entries = entries * block_scale(stream_key, dims, cuts, -0.22, 0.18)
    return jnp.clip(entries, -limit, limit).astype(held_as)


def setup_inputs(seed: int = 0) -> dict:
    arg_keys = jax.random.split(jax.random.key(seed), 7)
    return {
        "grid_fields": noise(arg_keys[0], (LEV, FIELDS, SLOTS, 2 * TILE), 1.0, 6.0, ((2, 32),), jnp.float32),
        "diffusivity": jnp.clip(jnp.exp(math.log(20.0) - 5.9953784 * jax.random.uniform(arg_keys[1], (LEV - 1, SLOTS, 2 * TILE), jnp.float32) ** block_scale(arg_keys[1], (LEV - 1, SLOTS, 2 * TILE), ((1, 32),), -0.2, 0.2)), 0.049804688, 20.0).astype(jnp.bfloat16),
        "tile_map": draw_tile_map(jax.random.fold_in(arg_keys[6], 71), 0),
        "pair_order": draw_pair_order(jax.random.fold_in(arg_keys[6], 71), 0),
        "m_order": jax.random.permutation(arg_keys[4], NMP).astype(jnp.int32),
        "legendre": noise(arg_keys[5], (NMP, NCOEF, NPAIR), NPAIR ** -0.5, 0.25, ((0, 8),)),
    }


TWO_PI = 6.283185307179586

def diffuse(fields, diffusivity):
    coefficient = diffusivity.astype(jnp.float32)
    zero_row = jnp.zeros((1,) + coefficient.shape[1:], jnp.float32)
    lower_coefs = jnp.concatenate([zero_row, coefficient], axis=0)
    upper_coefs = jnp.concatenate([coefficient, zero_row], axis=0)

    def forward(carry, inputs):
        last_ratio, last_partial = carry
        column_value, lower_coef, upper_coef = inputs
        pivot_value = 1.0 + lower_coef + upper_coef - lower_coef * last_ratio
        new_ratio = upper_coef / pivot_value
        new_partial = (column_value + lower_coef[None] * last_partial) / pivot_value[None]
        return ((new_ratio, new_partial), (new_ratio, new_partial))
    start_state = (jnp.zeros(fields.shape[2:], jnp.float32), jnp.zeros(fields.shape[1:], jnp.float32))
    _, (ratios, partials) = lax.scan(forward, start_state, (fields, lower_coefs, upper_coefs))

    def backward(upper_value, inputs):
        ratio_now, partial_now = inputs
        solved = partial_now + ratio_now[None] * upper_value
        return (solved, solved)
    _, result = lax.scan(backward, jnp.zeros(fields.shape[1:], jnp.float32), (ratios, partials), reverse=True)
    return result

def pair_tables(pair_id):
    points = 4 * pair_id + 20
    count_float = points.astype(jnp.float32)
    wave_ids = jnp.arange(NM, dtype=jnp.int32)
    within = jnp.arange(TILE, dtype=jnp.int32)
    coarse_ids = jnp.arange(TILE // 16, dtype=jnp.int32) * 16
    fine_ids = jnp.arange(16, dtype=jnp.int32)
    starts = jnp.arange(BLK, dtype=jnp.int32) * TILE
    coarse_angle = TWO_PI * (coarse_ids[:, None] * wave_ids[None, :] % points).astype(jnp.float32) / count_float
    fine_angle = TWO_PI * (fine_ids[:, None] * wave_ids[None, :] % points).astype(jnp.float32) / count_float
    coarse_cos = jnp.cos(coarse_angle)[:, None, :]
    coarse_sin = jnp.sin(coarse_angle)[:, None, :]
    fine_cos = jnp.cos(fine_angle)[None, :, :]
    fine_sin = jnp.sin(fine_angle)[None, :, :]
    cos_table = (coarse_cos * fine_cos - coarse_sin * fine_sin).reshape(TILE, NM)
    sin_table = (coarse_sin * fine_cos + coarse_cos * fine_sin).reshape(TILE, NM)
    outer_angle = TWO_PI * (starts[:, None] * wave_ids[None, :] % points).astype(jnp.float32) / count_float
    phase_table = jnp.concatenate([cos_table, -sin_table], axis=1).astype(jnp.bfloat16)
    usable = starts[:, None] + within[None, :] < points
    return (phase_table, jnp.cos(outer_angle), jnp.sin(outer_angle), usable, 1.0 / jnp.sqrt(count_float))

def reference(grid_fields, diffusivity, tile_map, pair_order, m_order, legendre):
    diffused = diffuse(grid_fields, diffusivity).astype(jnp.bfloat16)
    cell_index = jnp.where(tile_map >= 0, tile_map, NPAIR * BLK)
    cell_grid = jnp.zeros((LEV, FIELDS, NPAIR * BLK, 2 * TILE), jnp.bfloat16)
    cell_grid = cell_grid.at[:, :, cell_index].set(diffused, mode='drop')
    cell_grid = jnp.moveaxis(cell_grid.reshape(LEV, FIELDS, NPAIR, BLK, 2, TILE), 2, 0)

    def one_pair(inputs):
        pair_id, block_data = inputs
        phase_table, twist_cos, twist_sin, usable, norm_scale = pair_tables(pair_id)
        masked = jnp.where(usable[None, None, :, None, :], block_data, jnp.zeros((), jnp.bfloat16))
        partial_value = jnp.einsum('lfbht,tm->bhflm', masked.astype(jnp.float32), phase_table.astype(jnp.float32), precision=lax.Precision.HIGHEST)
        real_part = partial_value[..., :NM]
        imag_part = partial_value[..., NM:]
        cos_twist = twist_cos[:, None, None, None, :]
        sin_twist = twist_sin[:, None, None, None, :]
        total_re = lax.optimization_barrier(jnp.sum(cos_twist * real_part + sin_twist * imag_part, axis=0)) * norm_scale
        total_im = lax.optimization_barrier(jnp.sum(cos_twist * imag_part - sin_twist * real_part, axis=0)) * norm_scale
        return jnp.stack([total_re, total_im], axis=1).astype(jnp.bfloat16)
    fourier = lax.map(one_pair, (jnp.arange(NPAIR, dtype=jnp.int32), cell_grid))
    north_part = fourier[:, 0].astype(jnp.float32)
    south_part = fourier[:, 1].astype(jnp.float32)
    symmetric = (north_part + south_part).astype(jnp.bfloat16)
    antisymmetric = (north_part - south_part).astype(jnp.bfloat16)

    def one_set(inputs):
        wave_pair, functions = inputs
        wave_picks = jnp.stack([wave_pair, NM - 1 - wave_pair]).astype(jnp.int32)
        sym_waves = jnp.take(symmetric, wave_picks, axis=4).astype(jnp.float32)
        anti_waves = jnp.take(antisymmetric, wave_picks, axis=4).astype(jnp.float32)
        table_float = functions.astype(jnp.float32)
        from_sym = jnp.einsum('ki,iaflw->waflk', table_float, sym_waves)
        from_anti = jnp.einsum('ki,iaflw->waflk', table_float, anti_waves)
        ordinal = jnp.arange(NM + 1, dtype=jnp.int32)
        first_wave = ordinal < NM - wave_pair
        even_low = ordinal % 2 == 0
        even_high = (ordinal - (NM - wave_pair)) % 2 == 0
        spectral_set = jnp.where(first_wave, jnp.where(even_low, from_sym[0], from_anti[0]), jnp.where(even_high, from_sym[1], from_anti[1]))
        degree = jnp.where(first_wave, wave_pair + ordinal, ordinal - 1).astype(jnp.float32)
        damping = 1.0 / (1.0 + 8.0 * degree * (degree + 1.0) / (NM * NM))
        damped = (spectral_set * damping).astype(jnp.bfloat16)
        selectors = jnp.stack([first_wave & even_low, first_wave & ~even_low, ~first_wave & even_high, ~first_wave & ~even_high], axis=0)
        masked_sets = jnp.where(selectors[:, None, None, None, :], damped[None], jnp.zeros((), jnp.bfloat16))
        rebuilt = jnp.einsum('ki,xaflk->xiafl', table_float, masked_sets.astype(jnp.float32))
        north_back = rebuilt[0::2] + rebuilt[1::2]
        south_back = rebuilt[0::2] - rebuilt[1::2]
        returned_part = jnp.stack([north_back, south_back], axis=2).astype(jnp.bfloat16)
        return (spectral_set, returned_part)
    spectral, rebuilt_all = lax.map(one_set, (m_order, legendre))
    fourier_out = jnp.transpose(rebuilt_all, (2, 3, 4, 5, 6, 1, 0)).reshape(NPAIR, 2, 2, FIELDS, LEV, NM)
    fourier_out = jnp.take(fourier_out, pair_order, axis=0)
    return (spectral, fourier_out)
```

```python
import functools

import jax
import jax.numpy as jnp
from jax import lax
from jax.experimental import pallas as pl
from jax.experimental.pallas import tpu as pltpu
from jax.sharding import PartitionSpec as P

TILE = 256
BLK = 11
LANE = 128
ROWS = 16
GROUP = 8
F32 = jnp.float32
BF16 = jnp.bfloat16
MIB = 1024 * 1024
CHUNKS = ((0, 1, 2, 3, 4),)


def params(mib):
    return pltpu.CompilerParams(vmem_limit_bytes=mib * MIB)


def cost(flops, moved):
    return pl.CostEstimate(flops=int(flops), bytes_accessed=int(moved), transcendentals=0)


def row_order(lf):
    full = 2 * lf
    head = full // 8 * 8
    rows = []
    for start in range(0, head, 8):
        for kind in range(2):
            rows += [(kind, start + i) for i in range(8)]
    rest = full - head
    assert 2 * rest == 8 and head == 8
    for kind in range(2):
        rows += [(kind, head + i) for i in range(rest)]
    return rows


def swap_blocks(items, width):
    items = list(items)
    lane = lax.broadcasted_iota(jnp.int32, items[0].shape, 1)
    step = 1
    while step < len(items):
        reach = width * step
        low = (lane & reach) == 0
        for i in range(len(items)):
            if i & step:
                continue
            first, second = items[i], items[i + step]
            items[i] = jnp.where(low, first, pltpu.roll(second, reach, 1))
            items[i + step] = jnp.where(low, pltpu.roll(first, LANE - reach, 1), second)
        step *= 2
    return items


def diffuse_kernel(share, x_ref, a_ref, o_ref):
    levels, fields = x_ref.shape[0], x_ref.shape[1]
    width = x_ref.shape[-1]
    for start in range(0, width, LANE):
        cut = pl.ds(start, LANE)
        coef = [a_ref[k, 0, :, cut].astype(F32) for k in range(levels - 1)]
        ratios = []
        partials = [[] for _ in range(fields)]
        for k in range(levels):
            if k == 0:
                pivot = 1.0 + coef[0]
            elif k == levels - 1:
                pivot = 1.0 + coef[k - 1] - coef[k - 1] * ratios[k - 1]
            else:
                pivot = 1.0 + coef[k - 1] + coef[k] - coef[k - 1] * ratios[k - 1]
            inverse = 1.0 / pivot
            if k < levels - 1:
                ratios.append(coef[k] * inverse)
            for f in range(fields):
                value = x_ref[k, f, 0, :, cut]
                if k:
                    value = value + coef[k - 1] * partials[f][k - 1]
                partials[f].append(value * inverse)
        for f in range(fields):
            solved = None
            for k in range(levels - 1, -1, -1):
                solved = partials[f][k] if solved is None else partials[f][k] + ratios[k] * solved
                o_ref[0, k // share, k % share, f, :, cut] = solved.astype(BF16)


def diffuse(grid_fields, diffusivity, waves, groups):
    levels, fields, slots, width = grid_fields.shape
    cap = slots // waves
    share = levels // groups
    x = grid_fields.reshape(levels, fields, waves, cap, width)
    a = diffusivity.reshape(levels - 1, waves, cap, width)
    return pl.pallas_call(
        functools.partial(diffuse_kernel, share),
        grid=(waves,),
        in_specs=[
            pl.BlockSpec((levels, fields, 1, cap, width), lambda w: (0, 0, w, 0, 0)),
            pl.BlockSpec((levels - 1, 1, cap, width), lambda w: (0, w, 0, 0)),
        ],
        out_specs=pl.BlockSpec((1, groups, share, fields, cap, width), lambda w: (w, 0, 0, 0, 0, 0)),
        out_shape=jax.ShapeDtypeStruct((waves, groups, share, fields, cap, width), BF16),
        compiler_params=params(32),
        cost_estimate=cost(40 * x.size, 6 * x.size + 2 * a.size),
        name="diffuse",
    )(x, a)


def turn(x, count, inverse):
    rest = x - count * jnp.floor(x * inverse)
    quarters = rest * (4.0 * inverse)
    near = jnp.floor(quarters + 0.5)
    angle = (quarters - near) * 1.5707963267948966
    square = angle * angle
    sine = angle * (
        1.0 + square * (-1.0 / 6 + square * (1.0 / 120 + square * (-1.0 / 5040 + square / 362880)))
    )
    cosine = 1.0 + square * (
        -0.5 + square * (1.0 / 24 + square * (-1.0 / 720 + square / 40320))
    )
    which = near.astype(jnp.int32) & 3
    odd = (which & 1) == 1
    cos_abs = jnp.where(odd, sine, cosine)
    sin_abs = jnp.where(odd, cosine, sine)
    cos_value = jnp.where((which == 1) | (which == 2), -cos_abs, cos_abs)
    sin_value = jnp.where(which >= 2, -sin_abs, sin_abs)
    return cos_value, sin_value


def table_kernel(count_ref, inverse_ref, scale_ref, m_ref, t_ref, w_ref, coarse_ref):
    pair = pl.program_id(0)
    count, inverse, scale = count_ref[pair], inverse_ref[pair], scale_ref[pair]
    step = lax.broadcasted_iota(jnp.int32, (ROWS, LANE), 0).astype(F32)
    for g in range(m_ref.shape[0]):
        base = step * m_ref[g]
        fine_cos, fine_sin = turn(base, count, inverse)
        coarse_cos, coarse_sin = turn(base * 16.0, count, inverse)
        outer_cos, outer_sin = turn(base * float(TILE), count, inverse)
        w_ref[g, 0, 0:ROWS, :] = outer_cos * scale
        w_ref[g, 0, ROWS : 2 * ROWS, :] = outer_sin * scale
        coarse_ref[0:ROWS, :] = coarse_cos
        coarse_ref[ROWS : 2 * ROWS, :] = coarse_sin
        for a in range(TILE // ROWS):
            u_cos = coarse_ref[pl.ds(a, 1), :]
            u_sin = coarse_ref[pl.ds(ROWS + a, 1), :]
            rows = pl.ds(a * ROWS, ROWS)
            t_ref[g, 0, rows, 0:LANE] = (u_cos * fine_cos - u_sin * fine_sin).astype(BF16)
            t_ref[g, 0, rows, LANE : 2 * LANE] = (-(u_sin * fine_cos + u_cos * fine_sin)).astype(BF16)


def phase_tables(local_pairs, m_lanes):
    pairs = local_pairs.shape[0]
    groups = m_lanes.shape[0]
    count = (4 * local_pairs + 20).astype(F32)
    return pl.pallas_call(
        table_kernel,
        grid_spec=pltpu.PrefetchScalarGridSpec(
            num_scalar_prefetch=3,
            grid=(pairs,),
            in_specs=[pl.BlockSpec((groups, 1, LANE), lambda p, *_: (0, 0, 0))],
            out_specs=[
                pl.BlockSpec((groups, 1, TILE, 2 * LANE), lambda p, *_: (0, p, 0, 0)),
                pl.BlockSpec((groups, 1, 2 * ROWS, LANE), lambda p, *_: (0, p, 0, 0)),
            ],
            scratch_shapes=[pltpu.VMEM((2 * ROWS, LANE), F32)],
        ),
        out_shape=[
            jax.ShapeDtypeStruct((groups, pairs, TILE, 2 * LANE), BF16),
            jax.ShapeDtypeStruct((groups, pairs, 2 * ROWS, LANE), F32),
        ],
        compiler_params=params(32),
        cost_estimate=cost(10 * groups * pairs * TILE * 2 * LANE, 2 * groups * pairs * TILE * 2 * LANE),
        name="tables",
    )(count, 1.0 / count, 1.0 / jnp.sqrt(count), m_lanes)


def gather_kernel(slot_ref, room_ref, x_ref, o_ref, s_ref):
    sources, share, fields, cap, width = x_ref.shape
    s_ref[...] = jnp.zeros_like(s_ref)

    def unpack(source, carry):
        for l in range(share):
            for f in range(fields):
                value = x_ref[source, l, f].astype(F32)
                for h in range(2):
                    for t in range(TILE // LANE):
                        start = h * TILE + t * LANE
                        first = source * (cap * ROWS) + (h * 8 + f * share + l)
                        s_ref[t, pl.ds(first, cap, stride=ROWS), :] = value[:, start : start + LANE]
        return carry

    lax.fori_loop(0, sources, unpack, 0)
    lane = lax.broadcasted_iota(jnp.int32, (ROWS, LANE), 1)

    def place(block, carry):
        first = pl.multiple_of(slot_ref[block] * ROWS, ROWS)
        room = room_ref[block]
        out = pl.multiple_of(block * ROWS, ROWS)
        for t in range(TILE // LANE):
            value = s_ref[t, pl.ds(first, ROWS), :]
            value = jnp.where(lane < room - t * LANE, value, 0.0)
            o_ref[pl.ds(out, ROWS), t * LANE : (t + 1) * LANE] = value.astype(BF16)
        return carry

    lax.fori_loop(0, o_ref.shape[0] // ROWS, place, 0, unroll=8)


def gather_tiles(arrived, slots, room):
    sources, share, fields, cap, width = arrived.shape
    blocks = slots.shape[0]
    return pl.pallas_call(
        gather_kernel,
        grid_spec=pltpu.PrefetchScalarGridSpec(
            num_scalar_prefetch=2,
            grid=(1,),
            in_specs=[pl.BlockSpec(arrived.shape, lambda i, *_: (0, 0, 0, 0, 0))],
            out_specs=pl.BlockSpec((blocks * ROWS, TILE), lambda i, *_: (0, 0)),
            scratch_shapes=[pltpu.VMEM((TILE // LANE, sources * cap * ROWS, LANE), F32)],
        ),
        out_shape=jax.ShapeDtypeStruct((blocks * ROWS, TILE), BF16),
        compiler_params=params(58),
        cost_estimate=cost(8 * arrived.size, 2 * arrived.size + 2 * blocks * ROWS * TILE),
        name="place_tiles",
    )(slots, room, arrived)


def rows_kernel(blocks, lf, waves, pairs, x_ref, t_ref, w_ref, o_ref, f_ref):
    stage = pl.program_id(1)
    first = 0
    for k, count in enumerate(blocks):

        def one(first=first, count=count, k=k):
            for i in range(GROUP):
                begin = (first + i * count) * ROWS
                y = jnp.dot(
                    x_ref[begin : begin + count * ROWS, :], t_ref[0, i], preferred_element_type=F32
                )
                re = im = None
                for b in range(count):
                    y_re = y[b * ROWS : (b + 1) * ROWS, 0:LANE]
                    y_im = y[b * ROWS : (b + 1) * ROWS, LANE : 2 * LANE]
                    w_cos = w_ref[0, i, b : b + 1, :]
                    w_sin = w_ref[0, i, ROWS + b : ROWS + b + 1, :]
                    add_re = w_cos * y_re + w_sin * y_im
                    add_im = w_cos * y_im - w_sin * y_re
                    re = add_re if re is None else re + add_re
                    im = add_im if im is None else im + add_im
                j = k * GROUP + i
                for a, part in enumerate((re, im)):
                    part = part.astype(BF16).astype(F32)
                    north, south = part[0:8], part[8:16]
                    for s, total in enumerate((north + south, north - south)):
                        start = (s * 2 * lf + a * lf) * pairs + j
                        f_ref[pl.ds(start, lf, stride=pairs), :] = total[0:lf]

        pl.when(stage == k)(one)
        first += count * GROUP

    def pack():
        order = row_order(lf)
        piece = 16 if pairs % 16 == 0 else pairs
        for cg in range(-(-len(order) // waves)):
            for start in range(0, pairs, piece):
                items = []
                for p in range(cg * waves, (cg + 1) * waves):
                    if p < len(order):
                        kind, row = order[p]
                        items.append(f_ref[pl.ds((kind * 2 * lf + row) * pairs + start, piece), :])
                    else:
                        items.append(jnp.zeros((piece, LANE), F32))
                for d, value in enumerate(swap_blocks(items, LANE // waves)):
                    o_ref[
                        pl.ds(d * pairs + start, piece), cg * LANE : (cg + 1) * LANE
                    ] = value.astype(BF16)

    pl.when(stage == len(blocks) - 1)(pack)


def rows_to_waves(tiles, table, twist, blocks, lf, waves, chunk):
    pairs = table.shape[1]
    cgs = -(-4 * lf // waves)
    g0, ng = chunk[0], len(chunk)
    stages = len(blocks)
    return pl.pallas_call(
        functools.partial(rows_kernel, blocks, lf, waves, pairs),
        grid=(ng, stages),
        in_specs=[
            pl.BlockSpec(tiles.shape, lambda g, k: (0, 0)),
            pl.BlockSpec((1, GROUP, TILE, 2 * LANE), lambda g, k: (g0 + g, k, 0, 0)),
            pl.BlockSpec((1, GROUP, 2 * ROWS, LANE), lambda g, k: (g0 + g, k, 0, 0)),
        ],
        out_specs=pl.BlockSpec((waves * pairs, cgs * LANE), lambda g, k: (0, g)),
        out_shape=jax.ShapeDtypeStruct((waves * pairs, ng * cgs * LANE), BF16),
        scratch_shapes=[pltpu.VMEM((4 * lf * pairs, LANE), F32)],
        compiler_params=params(48),
        cost_estimate=cost(
            ng * 2 * tiles.size * 2 * LANE, 2 * tiles.size + ng * (2 * table[0].size + 4 * twist[0].size)
        ),
        name="rows_to_waves",
    )(tiles, table, twist)


def legendre_kernel(g0, per_group, waves, lf, total, own_ref, r_ref, p_ref, l_ref, *rest):
    s_ref, o_ref, d_ref, b_ref = rest[-4:]
    width = LANE // waves
    group, stage = pl.program_id(0), pl.program_id(1)
    many = l_ref.shape[0]
    order = row_order(lf)
    tiles = len(order) // 8
    rows = r_ref.shape[1]
    coefs = l_ref.shape[1]
    lanes = l_ref.shape[2] // LANE

    def begin():
        value = lax.dot_general(
            r_ref[...], p_ref[...], (((0,), (0,)), ((), ())), preferred_element_type=F32
        )
        for t in range(lanes):
            d_ref[t] = value[:, t * LANE : (t + 1) * LANE]
        if rows > len(order) * width:
            b_ref[...] = jnp.zeros_like(b_ref)

    pl.when(stage == 0)(begin)
    ordinal = lax.broadcasted_iota(jnp.int32, (8, coefs), 1)
    low_rows = lax.broadcasted_iota(jnp.int32, (8, coefs), 0) < 4

    for i in range(many):
        local = stage * many + i
        q = own_ref[(g0 + group) * per_group + local]

        def where_rows(w, tile, local=local):
            p = tile * 8
            start = p // waves * LANE + p % waves * width + 2 * local + w
            return pl.ds(start, 8, stride=width)

        picked = []
        for w in range(2):
            for tile in range(tiles):
                cut = where_rows(w, tile)
                picked.append(jnp.concatenate([d_ref[t, cut, :] for t in range(lanes)], axis=1))
        left = jnp.concatenate(picked, axis=0).astype(BF16)
        forward = lax.dot_general(
            left, l_ref[i], (((1,), (1,)), ((), ())), preferred_element_type=F32
        )
        split = total - q
        low = ordinal < split
        even = jnp.where(low, ordinal & 1, (ordinal - split) & 1) == 0
        chosen = [
            jnp.where(low, forward[t * 8 : t * 8 + 8], forward[(tiles + t) * 8 : (tiles + t) * 8 + 8])
            for t in range(tiles)
        ]
        head = jnp.where(even, chosen[0], chosen[1])
        tail = jnp.where(even, chosen[2], pltpu.roll(chosen[2], 4, 0))
        s_ref[i, 0:8, :] = head
        s_ref[i, 8:12, :] = tail[0:4]
        degree = jnp.where(low, q + ordinal, ordinal - 1).astype(F32)
        damping = 1.0 / (1.0 + 8.0 * degree * (degree + 1.0) / (total * total))
        head = head * damping
        tail = tail * damping
        tail = jnp.where(low_rows, tail, pltpu.roll(tail, 4, 0))
        parts = [head, jnp.where(even, head, -head), jnp.where(even | low_rows, tail, -tail)]
        back = jnp.concatenate(
            [jnp.where(low, x, 0.0) for x in parts] + [jnp.where(low, 0.0, x) for x in parts], axis=0
        ).astype(BF16)
        rebuilt = jnp.dot(back, l_ref[i], preferred_element_type=F32)
        for w in range(2):
            for tile in range(tiles):
                row = (w * tiles + tile) * 8
                cut = where_rows(w, tile)
                for t in range(lanes):
                    b_ref[t, cut, :] = rebuilt[row : row + 8, t * LANE : (t + 1) * LANE]

    def end():
        value = jnp.concatenate([b_ref[t].astype(BF16) for t in range(lanes)], axis=1)
        o_ref[...] = lax.dot_general(
            p_ref[...], value, (((1,), (1,)), ((), ())), preferred_element_type=F32
        ).astype(BF16)

    pl.when(stage == pl.num_programs(1) - 1)(end)


def legendre_both(received, places, legendre, own_sets, lf, waves, chunk, spectral):
    sets, coefs, pair_total = legendre.shape
    cgs = -(-4 * lf // waves)
    rows = cgs * LANE
    per_group = LANE // waves // 2
    many = 4
    stages = per_group // many
    g0, ng = chunk[0], len(chunk)
    block = lambda g, k, *_: ((g0 + g) * stages + k, 0, 0)
    in_specs = [
        pl.BlockSpec((pair_total, rows), lambda g, k, *_: (0, g)),
        pl.BlockSpec((pair_total, pair_total), lambda g, k, *_: (0, 0)),
        pl.BlockSpec((many, coefs, pair_total), block),
    ]
    operands = [own_sets, received, places, legendre]
    aliases = {}
    if spectral is not None:
        in_specs.append(pl.BlockSpec(memory_space=pl.ANY))
        operands.append(spectral)
        aliases = {4: 0}
    return pl.pallas_call(
        functools.partial(legendre_kernel, g0, per_group, waves, lf, coefs - 1),
        grid_spec=pltpu.PrefetchScalarGridSpec(
            num_scalar_prefetch=1,
            grid=(ng, stages),
            in_specs=in_specs,
            out_specs=[
                pl.BlockSpec((many, 2 * lf, coefs), block),
                pl.BlockSpec((pair_total, rows), lambda g, k, *_: (0, g)),
            ],
            scratch_shapes=[
                pltpu.VMEM((pair_total // LANE, rows, LANE), F32),
                pltpu.VMEM((pair_total // LANE, rows, LANE), F32),
            ],
        ),
        out_shape=[
            jax.ShapeDtypeStruct((sets, 2 * lf, coefs), F32),
            jax.ShapeDtypeStruct((pair_total, ng * rows), BF16),
        ],
        input_output_aliases=aliases,
        compiler_params=params(48),
        cost_estimate=cost(
            ng * per_group * 4 * 48 * coefs * pair_total, ng * per_group * 2 * coefs * pair_total
        ),
        name="legendre",
    )(*operands)


def unpack_kernel(order, lf, *refs):
    perm_ref, o_ref, g_ref = refs[-3:]
    parts = refs[:-3]
    sources, piece = parts[0].shape[0], parts[0].shape[1]
    width = LANE // sources
    cgs = -(-len(order) // sources)
    many = 4 * lf
    g = 0
    for ref in parts:
        for local in range(ref.shape[2] // (cgs * LANE)):
            for cg in range(cgs):
                start = (local * cgs + cg) * LANE
                items = [ref[s, :, start : start + LANE].astype(F32) for s in range(sources)]
                for d, value in enumerate(swap_blocks(items, width)):
                    p = cg * sources + d
                    if p < len(order):
                        kind, row = order[p]
                        g_ref[g, pl.ds(kind * 2 * lf + row, piece, stride=many), :] = value
            g += 1
    left = jnp.concatenate([g_ref[t].astype(BF16) for t in range(g)], axis=1)
    o_ref[...] = jnp.dot(left, perm_ref[...], preferred_element_type=F32).astype(BF16)


def unpack_rows(parts, perm, lf, waves):
    pairs = parts[0].shape[0] // waves
    piece = 16 if pairs % 16 == 0 else pairs
    total = perm.shape[0]
    shaped = [x.reshape(waves, pairs, x.shape[1]) for x in parts]
    size = sum(x.size for x in shaped)
    return pl.pallas_call(
        functools.partial(unpack_kernel, row_order(lf), lf),
        grid=(pairs // piece,),
        in_specs=[pl.BlockSpec((waves, piece, x.shape[2]), lambda j: (0, j, 0)) for x in shaped]
        + [pl.BlockSpec((total, total), lambda j: (0, 0))],
        out_specs=pl.BlockSpec((piece * 4 * lf, total), lambda j: (j, 0)),
        out_shape=jax.ShapeDtypeStruct((pairs * 4 * lf, total), BF16),
        scratch_shapes=[pltpu.VMEM((total // LANE, piece * 4 * lf, LANE), F32)],
        compiler_params=params(32),
        cost_estimate=cost(2 * size * total, 4 * size),
        name="unpack",
    )(*shaped, perm)


def body(grid_fields, diffusivity, tile_map, pair_order, m_order, legendre):
    waves = lax.axis_size("wave")
    groups = lax.axis_size("lev")
    me = lax.axis_index("wave")
    levels, fields, slots, width = grid_fields.shape
    cap = slots // waves
    share = levels // groups
    lf = share * fields
    pair_total = pair_order.shape[0]
    pairs = pair_total // waves
    set_total = m_order.shape[0]
    sets = set_total // waves
    waves_total = 2 * set_total
    lane_groups = waves_total // LANE
    run = LANE // waves

    outgoing = diffuse(grid_fields, diffusivity, waves, groups)
    outgoing = outgoing.reshape(waves * groups, share, fields, cap, width)
    arrived = lax.all_to_all(outgoing, ("wave", "lev"), 0, 0, tiled=True)

    local_pairs = lax.dynamic_slice_in_dim(pair_order, me * pairs, pairs)
    picks = jnp.stack([m_order, waves_total - 1 - m_order], axis=1)
    m_lanes = picks.reshape(waves, lane_groups, run).transpose(1, 0, 2)
    m_lanes = m_lanes.reshape(lane_groups, 1, LANE).astype(F32)
    table, twist = phase_tables(local_pairs, m_lanes)

    stages = pairs // GROUP
    blocks = []
    for k in range(stages):
        largest = waves * (k * GROUP + GROUP - 1) + waves - 1
        blocks.append(min(BLK, -(-(4 * largest + 20) // TILE)))
    pair_at = [k * GROUP + i for k in range(stages) for i in range(GROUP) for _ in range(blocks[k])]
    block_at = [b for k in range(stages) for i in range(GROUP) for b in range(blocks[k])]
    pair_at = jnp.asarray(pair_at, jnp.int32)
    block_at = jnp.asarray(block_at, jnp.int32)
    pair_ids = jnp.take(local_pairs, pair_at)
    wanted = pair_ids * BLK + block_at
    room = 4 * pair_ids + 20 - block_at * TILE
    catalog = tile_map.reshape(waves, groups, waves, cap)
    own = lax.dynamic_index_in_dim(catalog, me, axis=2, keepdims=False).reshape(-1)
    slot_ids = jnp.arange(own.shape[0], dtype=jnp.int32)
    found = jnp.where(own[None, :] == wanted[:, None], slot_ids[None, :], 0)
    slot_of = jnp.max(found, axis=1)

    tiles = gather_tiles(arrived, slot_of, room)

    places = (pair_order[:, None] == jnp.arange(pair_total, dtype=jnp.int32)[None, :]).astype(BF16)
    own_sets = lax.dynamic_slice_in_dim(m_order, me * sets, sets)
    lane = jnp.arange(waves_total, dtype=jnp.int32)
    spot = lane // LANE * run + lane % run
    column = spot % 2 * set_total + lane % LANE // run * sets + spot // 2
    perm = (column[:, None] == lane[None, :]).astype(BF16)

    received = []
    for chunk in CHUNKS:
        sent = rows_to_waves(tiles, table, twist, tuple(blocks), lf, waves, chunk)
        received.append(lax.all_to_all(sent, "wave", 0, 0, tiled=True))
    spectral = None
    returned = []
    for chunk, part in zip(CHUNKS, received):
        spectral, back = legendre_both(
            part, places, legendre, own_sets, lf, waves, chunk, spectral
        )
        returned.append(lax.all_to_all(back, "wave", 0, 0, tiled=True))
    fourier_out = unpack_rows(returned, perm, lf, waves)
    spectral = spectral.reshape(sets, 2, fields, share, legendre.shape[1])
    fourier_out = fourier_out.reshape(pairs, 2, 2, fields, share, waves_total)
    return spectral, fourier_out


def solution(mesh):
    return jax.shard_map(
        body,
        mesh=mesh,
        in_specs=(
            P(None, None, ("wave", "lev"), None),
            P(None, ("wave", "lev"), None),
            P(),
            P(),
            P(),
            P("wave", None, None),
        ),
        out_specs=(P("wave", None, None, "lev", None), P("wave", None, None, None, "lev", None)),
        check_vma=False,
    )
```

```python
import functools

import jax
import jax.numpy as jnp
from jax import lax
from jax.experimental import pallas as pl
from jax.experimental.pallas import tpu as pltpu
from jax.sharding import PartitionSpec as P

TILE = 256
BLK = 11
SPAN = 17
LANE = 128
ROWS = 16
F32 = jnp.float32
BF16 = jnp.bfloat16
MIB = 1024 * 1024
STEPS = (4, 8, 11)
CHUNKS = (2, 3)


def group_of(pairs):
    return 16 if pairs % 16 == 0 else 8


def params(mib):
    return pltpu.CompilerParams(vmem_limit_bytes=mib * MIB)


def cost(flops, moved):
    return pl.CostEstimate(flops=int(flops), bytes_accessed=int(moved), transcendentals=0)


def row_order(lf):
    full = 2 * lf
    head = full // 8 * 8
    rows = []
    for start in range(0, head, 8):
        for kind in range(2):
            rows += [(kind, start + i) for i in range(8)]
    rest = full - head
    assert 2 * rest == 8 and head == 8
    for kind in range(2):
        rows += [(kind, head + i) for i in range(rest)]
    return rows


def swap_blocks(items, width):
    items = list(items)
    lane = lax.broadcasted_iota(jnp.int32, items[0].shape, 1)
    step = 1
    while step < len(items):
        reach = width * step
        low = (lane & reach) == 0
        for i in range(len(items)):
            if i & step:
                continue
            first, second = items[i], items[i + step]
            items[i] = jnp.where(low, first, pltpu.roll(second, reach, 1))
            items[i + step] = jnp.where(low, pltpu.roll(first, LANE - reach, 1), second)
        step *= 2
    return items


def diffuse_kernel(share, x_ref, a_ref, o_ref):
    levels, fields = x_ref.shape[0], x_ref.shape[1]
    width = x_ref.shape[-1]
    for start in range(0, width, LANE):
        cut = pl.ds(start, LANE)
        coef = [a_ref[k, 0, :, cut].astype(F32) for k in range(levels - 1)]
        ratios = []
        partials = [[] for _ in range(fields)]
        for k in range(levels):
            if k == 0:
                pivot = 1.0 + coef[0]
            elif k == levels - 1:
                pivot = 1.0 + coef[k - 1] - coef[k - 1] * ratios[k - 1]
            else:
                pivot = 1.0 + coef[k - 1] + coef[k] - coef[k - 1] * ratios[k - 1]
            inverse = 1.0 / pivot
            if k < levels - 1:
                ratios.append(coef[k] * inverse)
            for f in range(fields):
                value = x_ref[k, f, 0, :, cut]
                if k:
                    value = value + coef[k - 1] * partials[f][k - 1]
                partials[f].append(value * inverse)
        for f in range(fields):
            solved = None
            for k in range(levels - 1, -1, -1):
                solved = partials[f][k] if solved is None else partials[f][k] + ratios[k] * solved
                o_ref[0, k // share, k % share, f, :, cut] = solved.astype(BF16)


def diffuse(grid_fields, diffusivity, waves, groups):
    levels, fields, slots, width = grid_fields.shape
    cap = slots // waves
    share = levels // groups
    x = grid_fields.reshape(levels, fields, waves, cap, width)
    a = diffusivity.reshape(levels - 1, waves, cap, width)
    return pl.pallas_call(
        functools.partial(diffuse_kernel, share),
        grid=(waves,),
        in_specs=[
            pl.BlockSpec((levels, fields, 1, cap, width), lambda w: (0, 0, w, 0, 0)),
            pl.BlockSpec((levels - 1, 1, cap, width), lambda w: (0, w, 0, 0)),
        ],
        out_specs=pl.BlockSpec((1, groups, share, fields, cap, width), lambda w: (w, 0, 0, 0, 0, 0)),
        out_shape=jax.ShapeDtypeStruct((waves, groups, share, fields, cap, width), BF16),
        compiler_params=params(60),
        cost_estimate=cost(40 * x.size, 6 * x.size + 2 * a.size),
        name="diffuse",
    )(x, a)


def turn(x, count, inverse):
    rest = x - count * jnp.floor(x * inverse)
    quarters = rest * (4.0 * inverse)
    near = jnp.floor(quarters + 0.5)
    angle = (quarters - near) * 1.5707963267948966
    square = angle * angle
    sine = angle * (
        1.0 + square * (-1.0 / 6 + square * (1.0 / 120 + square * (-1.0 / 5040 + square / 362880)))
    )
    cosine = 1.0 + square * (
        -0.5 + square * (1.0 / 24 + square * (-1.0 / 720 + square / 40320))
    )
    which = near.astype(jnp.int32) & 3
    odd = (which & 1) == 1
    cos_abs = jnp.where(odd, sine, cosine)
    sin_abs = jnp.where(odd, cosine, sine)
    cos_value = jnp.where((which == 1) | (which == 2), -cos_abs, cos_abs)
    sin_value = jnp.where(which >= 2, -sin_abs, sin_abs)
    return cos_value, sin_value


def table_kernel(chunks, count_ref, inverse_ref, scale_ref, m_ref, *refs):
    group = refs[0].shape[1]
    coarse_ref = refs[-1]
    step = lax.broadcasted_iota(jnp.int32, (ROWS, LANE), 0).astype(F32)
    spots = [(c, g) for c, size in enumerate(chunks) for g in range(size)]

    def one(i, carry):
        pair = pl.program_id(0) * group + i
        count, inverse, scale = count_ref[pair], inverse_ref[pair], scale_ref[pair]
        for at, (c, g) in enumerate(spots):
            t_ref, w_ref = refs[2 * c], refs[2 * c + 1]
            base = step * m_ref[at]
            fine_cos, fine_sin = turn(base, count, inverse)
            coarse_cos, coarse_sin = turn(base * 16.0, count, inverse)
            outer_cos, outer_sin = turn(base * float(TILE), count, inverse)
            w_ref[g, i, 0:ROWS, :] = outer_cos * scale
            w_ref[g, i, ROWS : 2 * ROWS, :] = outer_sin * scale
            coarse_ref[at, 0:ROWS, :] = coarse_cos
            coarse_ref[at, ROWS : 2 * ROWS, :] = coarse_sin
            for a in range(TILE // ROWS):
                u_cos = coarse_ref[at, pl.ds(a, 1), :]
                u_sin = coarse_ref[at, pl.ds(ROWS + a, 1), :]
                rows = pl.ds(a * ROWS, ROWS)
                t_ref[g, i, rows, 0:LANE] = (u_cos * fine_cos - u_sin * fine_sin).astype(BF16)
                t_ref[g, i, rows, LANE : 2 * LANE] = (-(u_sin * fine_cos + u_cos * fine_sin)).astype(BF16)
        return carry

    lax.fori_loop(0, group, one, 0)


def phase_tables(local_pairs, m_lanes, chunks):
    pairs = local_pairs.shape[0]
    groups = m_lanes.shape[0]
    group = group_of(pairs)
    count = (4 * local_pairs + 20).astype(F32)
    specs, shapes = [], []
    for ng in chunks:
        specs.append(pl.BlockSpec((ng, group, TILE, 2 * LANE), lambda p, *_: (0, p, 0, 0)))
        specs.append(pl.BlockSpec((ng, group, 2 * ROWS, LANE), lambda p, *_: (0, p, 0, 0)))
        shapes.append(jax.ShapeDtypeStruct((ng, pairs, TILE, 2 * LANE), BF16))
        shapes.append(jax.ShapeDtypeStruct((ng, pairs, 2 * ROWS, LANE), F32))
    return pl.pallas_call(
        functools.partial(table_kernel, chunks),
        grid_spec=pltpu.PrefetchScalarGridSpec(
            num_scalar_prefetch=3,
            grid=(pairs // group,),
            in_specs=[pl.BlockSpec((groups, 1, LANE), lambda p, *_: (0, 0, 0))],
            out_specs=specs,
            scratch_shapes=[pltpu.VMEM((groups, 2 * ROWS, LANE), F32)],
        ),
        out_shape=shapes,
        compiler_params=params(48),
        cost_estimate=cost(10 * groups * pairs * TILE * 2 * LANE, 2 * groups * pairs * TILE * 2 * LANE),
        name="tables",
    )(count, 1.0 / count, 1.0 / jnp.sqrt(count), m_lanes)


def gather_kernel(group, slot_ref, room_ref, x_ref, ahead_ref, o_ref, s_ref):
    del ahead_ref
    sources, share, fields, cap, width = x_ref.shape
    def unpack(source, carry):
        for l in range(share):
            for f in range(fields):
                value = x_ref[source, l, f].astype(F32)
                for h in range(2):
                    for t in range(TILE // LANE):
                        start = h * TILE + t * LANE
                        first = source * (cap * SPAN) + (h * 8 + f * share + l)
                        s_ref[t, pl.ds(first, cap, stride=SPAN), :] = value[:, start : start + LANE]
        return carry

    lax.fori_loop(0, sources, unpack, 0)
    lane = lax.broadcasted_iota(jnp.int32, (ROWS, LANE), 1)

    def place(batch, carry):
        for i in range(group):
            block = batch * group + i
            first, room = slot_ref[block] * SPAN, room_ref[block]
            rows = pl.ds(pl.multiple_of(block * ROWS, ROWS), ROWS)
            for t in range(TILE // LANE):
                value = s_ref[t, pl.ds(first, ROWS), :]
                value = jnp.where(lane < room - t * LANE, value, 0.0)
                o_ref[rows, t * LANE : (t + 1) * LANE] = value.astype(BF16)
        return carry

    lax.fori_loop(0, o_ref.shape[0] // (ROWS * group), place, 0)


def gather_tiles(arrived, slots, room, ahead):
    sources, share, fields, cap, width = arrived.shape
    blocks = slots.shape[0]
    return pl.pallas_call(
        functools.partial(gather_kernel, 16 if blocks % 16 == 0 else 8),
        grid_spec=pltpu.PrefetchScalarGridSpec(
            num_scalar_prefetch=2,
            grid=(1,),
            in_specs=[
                pl.BlockSpec(arrived.shape, lambda i, *_: (0, 0, 0, 0, 0)),
                pl.BlockSpec(memory_space=pl.ANY),
            ],
            out_specs=pl.BlockSpec((blocks * ROWS, TILE), lambda i, *_: (0, 0)),
            scratch_shapes=[pltpu.VMEM((TILE // LANE, sources * cap * SPAN, LANE), F32)],
        ),
        out_shape=jax.ShapeDtypeStruct((blocks * ROWS, TILE), BF16),
        compiler_params=params(58),
        cost_estimate=cost(8 * arrived.size, 2 * arrived.size + 2 * blocks * ROWS * TILE),
        name="place_tiles",
    )(slots, room, arrived, ahead)


def rows_kernel(blocks, lf, waves, pairs, x_ref, t_ref, w_ref, o_ref, f_ref):
    stage = pl.program_id(0)
    many, group = t_ref.shape[:2]
    order = row_order(lf)
    cgs = -(-len(order) // waves)
    first = 0
    begin = 0
    while begin < len(blocks):
        count = blocks[begin]
        end = begin + blocks.count(count)

        def bucket(first=first, begin=begin, count=count):
            base = first + (stage - begin) * (group * count)

            def one(g, carry):
                for i in range(group):
                    top = pl.multiple_of((base + i * count) * ROWS, ROWS)
                    rows = pl.ds(top, count * ROWS)
                    y = jnp.dot(x_ref[rows, :], t_ref[g, i], preferred_element_type=F32)
                    re = im = None
                    for b in range(count):
                        y_re = y[b * ROWS : (b + 1) * ROWS, 0:LANE]
                        y_im = y[b * ROWS : (b + 1) * ROWS, LANE : 2 * LANE]
                        w_cos = w_ref[g, i, b : b + 1, :]
                        w_sin = w_ref[g, i, ROWS + b : ROWS + b + 1, :]
                        add_re = w_cos * y_re + w_sin * y_im
                        add_im = w_cos * y_im - w_sin * y_re
                        re = add_re if re is None else re + add_re
                        im = add_im if im is None else im + add_im
                    j = stage * group + i
                    for a, part in enumerate((re, im)):
                        part = part.astype(BF16).astype(F32)
                        north, south = part[0:8], part[8:16]
                        for s, total in enumerate((north + south, north - south)):
                            start = (s * 2 * lf + a * lf) * pairs + j
                            f_ref[g, pl.ds(start, lf, stride=pairs), :] = total[0:lf]
                return carry

            lax.fori_loop(0, many, one, 0)

        pl.when((stage >= begin) & (stage < end))(bucket)
        first += count * group * (end - begin)
        begin = end

    piece = 16 if pairs % 16 == 0 else pairs

    def pack():
        def one(step, carry):
            g, start = step // (pairs // piece), step % (pairs // piece) * piece
            for cg in range(cgs):
                items = []
                for p in range(cg * waves, (cg + 1) * waves):
                    if p < len(order):
                        kind, row = order[p]
                        top = pl.multiple_of((kind * 2 * lf + row) * pairs + start, 8)
                        items.append(f_ref[g, pl.ds(top, piece), :])
                    else:
                        items.append(jnp.zeros((piece, LANE), F32))
                lane = pl.multiple_of((g * cgs + cg) * LANE, LANE)
                for d, value in enumerate(swap_blocks(items, LANE // waves)):
                    top = pl.multiple_of(d * pairs + start, piece)
                    o_ref[pl.ds(top, piece), pl.ds(lane, LANE)] = value.astype(BF16)
            return carry

        lax.fori_loop(0, many * (pairs // piece), one, 0, unroll=pairs // piece)

    pl.when(stage == len(blocks) - 1)(pack)


def rows_to_waves(tiles, table, twist, blocks, lf, waves):
    ng, pairs = table.shape[:2]
    group = group_of(pairs)
    cgs = -(-4 * lf // waves)
    return pl.pallas_call(
        functools.partial(rows_kernel, blocks, lf, waves, pairs),
        grid=(len(blocks),),
        in_specs=[
            pl.BlockSpec(tiles.shape, lambda k: (0, 0)),
            pl.BlockSpec((ng, group, TILE, 2 * LANE), lambda k: (0, k, 0, 0)),
            pl.BlockSpec((ng, group, 2 * ROWS, LANE), lambda k: (0, k, 0, 0)),
        ],
        out_specs=pl.BlockSpec((waves * pairs, ng * cgs * LANE), lambda k: (0, 0)),
        out_shape=jax.ShapeDtypeStruct((waves * pairs, ng * cgs * LANE), BF16),
        scratch_shapes=[pltpu.VMEM((ng, 4 * lf * pairs, LANE), F32)],
        compiler_params=params(56),
        cost_estimate=cost(
            ng * 2 * tiles.size * 2 * LANE, 2 * tiles.size + 2 * table.size + 4 * twist.size
        ),
        name="rows_to_waves",
    )(tiles, table, twist)


def legendre_kernel(g0, per_group, waves, lf, total, own_ref, r_ref, p_ref, l_ref, *rest):
    s_ref, o_ref, d_ref, b_ref = rest[-4:]
    width = LANE // waves
    group, stage = pl.program_id(0), pl.program_id(1)
    many = l_ref.shape[0]
    order = row_order(lf)
    tiles = len(order) // 8
    rows = r_ref.shape[1]
    coefs = l_ref.shape[1]
    lanes = l_ref.shape[2] // LANE

    def begin():
        value = lax.dot_general(
            r_ref[...], p_ref[...], (((0,), (0,)), ((), ())), preferred_element_type=F32
        )
        for t in range(lanes):
            d_ref[t] = value[:, t * LANE : (t + 1) * LANE]
        if rows > len(order) * width:
            b_ref[...] = jnp.zeros_like(b_ref)

    pl.when(stage == 0)(begin)
    ordinal = lax.broadcasted_iota(jnp.int32, (8, coefs), 1)
    low_rows = lax.broadcasted_iota(jnp.int32, (8, coefs), 0) < 4

    for i in range(many):
        local = stage * many + i
        q = own_ref[(g0 + group) * per_group + local]

        def where_rows(w, tile, local=local):
            p = tile * 8
            start = p // waves * LANE + p % waves * width + 2 * local + w
            return pl.ds(start, 8, stride=width)

        picked = []
        for w in range(2):
            for tile in range(tiles):
                cut = where_rows(w, tile)
                picked.append(jnp.concatenate([d_ref[t, cut, :] for t in range(lanes)], axis=1))
        left = jnp.concatenate(picked, axis=0).astype(BF16)
        forward = lax.dot_general(
            left, l_ref[i], (((1,), (1,)), ((), ())), preferred_element_type=F32
        )
        split = total - q
        low = ordinal < split
        even = jnp.where(low, ordinal & 1, (ordinal - split) & 1) == 0
        chosen = [
            jnp.where(low, forward[t * 8 : t * 8 + 8], forward[(tiles + t) * 8 : (tiles + t) * 8 + 8])
            for t in range(tiles)
        ]
        head = jnp.where(even, chosen[0], chosen[1])
        tail = jnp.where(even, chosen[2], pltpu.roll(chosen[2], 4, 0))
        s_ref[i, 0:8, :] = head
        s_ref[i, 8:12, :] = tail[0:4]
        degree = jnp.where(low, q + ordinal, ordinal - 1).astype(F32)
        damping = 1.0 / (1.0 + 8.0 * degree * (degree + 1.0) / (total * total))
        head = head * damping
        tail = tail * damping
        tail = jnp.where(low_rows, tail, pltpu.roll(tail, 4, 0))
        parts = [head, jnp.where(even, head, -head), jnp.where(even | low_rows, tail, -tail)]
        back = jnp.concatenate(
            [jnp.where(low, x, 0.0) for x in parts] + [jnp.where(low, 0.0, x) for x in parts], axis=0
        ).astype(BF16)
        rebuilt = jnp.dot(back, l_ref[i], preferred_element_type=F32)
        for w in range(2):
            for tile in range(tiles):
                row = (w * tiles + tile) * 8
                cut = where_rows(w, tile)
                for t in range(lanes):
                    b_ref[t, cut, :] = rebuilt[row : row + 8, t * LANE : (t + 1) * LANE]

    def end():
        value = jnp.concatenate([b_ref[t].astype(BF16) for t in range(lanes)], axis=1)
        o_ref[...] = lax.dot_general(
            p_ref[...], value, (((1,), (1,)), ((), ())), preferred_element_type=F32
        ).astype(BF16)

    pl.when(stage == pl.num_programs(1) - 1)(end)


def legendre_both(received, places, legendre, own_sets, lf, waves, chunk, spectral):
    sets, coefs, pair_total = legendre.shape
    cgs = -(-4 * lf // waves)
    rows = cgs * LANE
    per_group = LANE // waves // 2
    many = 4
    stages = per_group // many
    g0, ng = chunk
    block = lambda g, k, *_: ((g0 + g) * stages + k, 0, 0)
    in_specs = [
        pl.BlockSpec((pair_total, rows), lambda g, k, *_: (0, g)),
        pl.BlockSpec((pair_total, pair_total), lambda g, k, *_: (0, 0)),
        pl.BlockSpec((many, coefs, pair_total), block),
    ]
    operands = [own_sets, received, places, legendre]
    aliases = {}
    if spectral is not None:
        in_specs.append(pl.BlockSpec(memory_space=pl.ANY))
        operands.append(spectral)
        aliases = {4: 0}
    return pl.pallas_call(
        functools.partial(legendre_kernel, g0, per_group, waves, lf, coefs - 1),
        grid_spec=pltpu.PrefetchScalarGridSpec(
            num_scalar_prefetch=1,
            grid=(ng, stages),
            in_specs=in_specs,
            out_specs=[
                pl.BlockSpec((many, 2 * lf, coefs), block),
                pl.BlockSpec((pair_total, rows), lambda g, k, *_: (0, g)),
            ],
            scratch_shapes=[
                pltpu.VMEM((pair_total // LANE, rows, LANE), F32),
                pltpu.VMEM((pair_total // LANE, rows, LANE), F32),
            ],
        ),
        out_shape=[
            jax.ShapeDtypeStruct((sets, 2 * lf, coefs), F32),
            jax.ShapeDtypeStruct((pair_total, ng * rows), BF16),
        ],
        input_output_aliases=aliases,
        compiler_params=params(48),
        cost_estimate=cost(
            ng * per_group * 4 * 48 * coefs * pair_total, ng * per_group * 2 * coefs * pair_total
        ),
        name="legendre",
    )(*operands)


def unpack_kernel(order, lf, *refs):
    perm_ref, o_ref, g_ref = refs[-3:]
    parts = refs[:-3]
    sources, piece = parts[0].shape[0], parts[0].shape[1]
    cgs = -(-len(order) // sources)
    g = 0
    for ref in parts:
        for local in range(ref.shape[2] // (cgs * LANE)):
            for cg in range(cgs):
                start = (local * cgs + cg) * LANE
                items = [ref[s, :, start : start + LANE] for s in range(sources)]
                for d, value in enumerate(swap_blocks(items, LANE // sources)):
                    p = cg * sources + d
                    if p < len(order):
                        kind, row = order[p]
                        top = (kind * 2 * lf + row) * piece
                        g_ref[g, top : top + piece, :] = value
            g += 1
    left = jnp.concatenate([g_ref[t] for t in range(g)], axis=1)
    value = jnp.dot(left, perm_ref[...], preferred_element_type=F32).astype(BF16)
    o_ref[...] = value.reshape(o_ref.shape)


def unpack_rows(parts, perm, lf, waves):
    pairs = parts[0].shape[0] // waves
    piece = 16 if pairs % 16 == 0 else pairs
    total = perm.shape[0]
    shaped = [x.reshape(waves, pairs, x.shape[1]) for x in parts]
    size = sum(x.size for x in shaped)
    return pl.pallas_call(
        functools.partial(unpack_kernel, row_order(lf), lf),
        grid=(pairs // piece,),
        in_specs=[pl.BlockSpec((waves, piece, x.shape[2]), lambda j: (0, j, 0)) for x in shaped]
        + [
            pl.BlockSpec((total, total), lambda j: (0, 0)),
        ],
        out_specs=pl.BlockSpec((4 * lf, piece, total), lambda j: (0, j, 0)),
        out_shape=jax.ShapeDtypeStruct((4 * lf, pairs, total), BF16),
        scratch_shapes=[pltpu.VMEM((total // LANE, piece * 4 * lf, LANE), BF16)],
        compiler_params=params(32),
        cost_estimate=cost(2 * size * total, 4 * size),
        name="unpack",
    )(*shaped, perm)


def body(grid_fields, diffusivity, tile_map, pair_order, m_order, legendre):
    waves = lax.axis_size("wave")
    groups = lax.axis_size("lev")
    me = lax.axis_index("wave")
    levels, fields, slots, width = grid_fields.shape
    cap = slots // waves
    share = levels // groups
    lf = share * fields
    pair_total = pair_order.shape[0]
    pairs = pair_total // waves
    set_total = m_order.shape[0]
    sets = set_total // waves
    waves_total = 2 * set_total
    lane_groups = waves_total // LANE
    run = LANE // waves

    outgoing = diffuse(grid_fields, diffusivity, waves, groups)
    outgoing = outgoing.reshape(waves * groups, share, fields, cap, width)
    arrived = lax.all_to_all(outgoing, ("wave", "lev"), 0, 0, tiled=True)

    local_pairs = lax.dynamic_slice_in_dim(pair_order, me * pairs, pairs)
    picks = jnp.stack([m_order, waves_total - 1 - m_order], axis=1)
    m_lanes = picks.reshape(waves, lane_groups, run).transpose(1, 0, 2)
    m_lanes = m_lanes.reshape(lane_groups, 1, LANE).astype(F32)
    chunks = CHUNKS if sum(CHUNKS) == lane_groups else (lane_groups,)
    tables = phase_tables(local_pairs, m_lanes, chunks)

    group = group_of(pairs)
    stages = pairs // group
    blocks = []
    for k in range(stages):
        largest = waves * (k * group + group - 1) + waves - 1
        least = min(BLK, -(-(4 * largest + 20) // TILE))
        blocks.append(min(x for x in STEPS if x >= least))
    pair_at = [k * group + i for k in range(stages) for i in range(group) for _ in range(blocks[k])]
    block_at = [b for k in range(stages) for i in range(group) for b in range(blocks[k])]
    pair_at = jnp.asarray(pair_at, jnp.int32)
    block_at = jnp.asarray(block_at, jnp.int32)
    pair_ids = jnp.take(local_pairs, pair_at)
    wanted = pair_ids * BLK + block_at
    room = 4 * pair_ids + 20 - block_at * TILE
    catalog = tile_map.reshape(waves, groups, waves, cap)
    own = lax.dynamic_index_in_dim(catalog, me, axis=2, keepdims=False).reshape(-1)
    slot_ids = jnp.arange(own.shape[0], dtype=jnp.int32)
    found = jnp.where(own[None, :] == wanted[:, None], slot_ids[None, :], 0)
    slot_of = jnp.max(found, axis=1)

    tiles = gather_tiles(arrived, slot_of, room, legendre)

    places = (pair_order[:, None] == jnp.arange(pair_total, dtype=jnp.int32)[None, :]).astype(BF16)
    own_sets = lax.dynamic_slice_in_dim(m_order, me * sets, sets)
    lane = jnp.arange(waves_total, dtype=jnp.int32)
    spot = lane // LANE * run + lane % run
    column = spot % 2 * set_total + lane % LANE // run * sets + spot // 2
    perm = (column[:, None] == lane[None, :]).astype(BF16)

    received = []
    for c in range(len(chunks)):
        sent = rows_to_waves(
            tiles, tables[2 * c], tables[2 * c + 1], tuple(blocks), lf, waves
        )
        received.append(lax.all_to_all(sent, "wave", 0, 0, tiled=True))
    spectral = None
    returned = []
    begin = 0
    for ng, part in zip(chunks, received):
        spectral, back = legendre_both(
            part, places, legendre, own_sets, lf, waves, (begin, ng), spectral
        )
        begin += ng
        returned.append(lax.all_to_all(back, "wave", 0, 0, tiled=True))
    fourier_out = unpack_rows(returned, perm, lf, waves)
    spectral = spectral.reshape(sets, 2, fields, share, legendre.shape[1])
    fourier_out = fourier_out.transpose(1, 0, 2).reshape(pairs, 2, 2, fields, share, waves_total)
    return spectral, fourier_out


def solution(mesh):
    return jax.shard_map(
        body,
        mesh=mesh,
        in_specs=(
            P(None, None, ("wave", "lev"), None),
            P(None, ("wave", "lev"), None),
            P(),
            P(),
            P(),
            P("wave", None, None),
        ),
        out_specs=(P("wave", None, None, "lev", None), P("wave", None, None, None, "lev", None)),
        check_vma=False,
    )
```

```python
import functools

import jax
import jax.numpy as jnp
from jax import lax
from jax.experimental import pallas as pl
from jax.experimental.pallas import tpu as pltpu
from jax.sharding import PartitionSpec as P

TILE = 256
BLK = 11
SPAN = 17
LANE = 128
ROWS = 16
F32 = jnp.float32
BF16 = jnp.bfloat16
MIB = 1024 * 1024
CHUNKS = (2, 3)


def group_of(pairs):
    return 16 if pairs % 16 == 0 else 8


def params(mib):
    return pltpu.CompilerParams(vmem_limit_bytes=mib * MIB)


def cost(flops, moved):
    return pl.CostEstimate(flops=int(flops), bytes_accessed=int(moved), transcendentals=0)


def row_order(lf):
    full = 2 * lf
    head = full // 8 * 8
    rows = []
    for start in range(0, head, 8):
        for kind in range(2):
            rows += [(kind, start + i) for i in range(8)]
    rest = full - head
    assert 2 * rest == 8 and head == 8
    for kind in range(2):
        rows += [(kind, head + i) for i in range(rest)]
    return rows


def swap_blocks(items, width):
    items = list(items)
    lane = lax.broadcasted_iota(jnp.int32, items[0].shape, 1)
    step = 1
    while step < len(items):
        reach = width * step
        low = (lane & reach) == 0
        for i in range(len(items)):
            if i & step:
                continue
            first, second = items[i], items[i + step]
            items[i] = jnp.where(low, first, pltpu.roll(second, reach, 1))
            items[i + step] = jnp.where(low, pltpu.roll(first, LANE - reach, 1), second)
        step *= 2
    return items


def diffuse_kernel(share, x_ref, a_ref, o_ref):
    levels, fields = x_ref.shape[0], x_ref.shape[1]
    width = x_ref.shape[-1]
    for start in range(0, width, LANE):
        cut = pl.ds(start, LANE)
        coef = [a_ref[k, 0, :, cut].astype(F32) for k in range(levels - 1)]
        ratios = []
        partials = [[] for _ in range(fields)]
        for k in range(levels):
            if k == 0:
                pivot = 1.0 + coef[0]
            elif k == levels - 1:
                pivot = 1.0 + coef[k - 1] - coef[k - 1] * ratios[k - 1]
            else:
                pivot = 1.0 + coef[k - 1] + coef[k] - coef[k - 1] * ratios[k - 1]
            inverse = 1.0 / pivot
            if k < levels - 1:
                ratios.append(coef[k] * inverse)
            for f in range(fields):
                value = x_ref[k, f, 0, :, cut]
                if k:
                    value = value + coef[k - 1] * partials[f][k - 1]
                partials[f].append(value * inverse)
        for f in range(fields):
            solved = None
            for k in range(levels - 1, -1, -1):
                solved = partials[f][k] if solved is None else partials[f][k] + ratios[k] * solved
                o_ref[0, k // share, k % share, f, :, cut] = solved.astype(BF16)


def diffuse(grid_fields, diffusivity, waves, groups):
    levels, fields, slots, width = grid_fields.shape
    cap = slots // waves
    share = levels // groups
    x = grid_fields.reshape(levels, fields, waves, cap, width)
    a = diffusivity.reshape(levels - 1, waves, cap, width)
    return pl.pallas_call(
        functools.partial(diffuse_kernel, share),
        grid=(waves,),
        in_specs=[
            pl.BlockSpec((levels, fields, 1, cap, width), lambda w: (0, 0, w, 0, 0)),
            pl.BlockSpec((levels - 1, 1, cap, width), lambda w: (0, w, 0, 0)),
        ],
        out_specs=pl.BlockSpec((1, groups, share, fields, cap, width), lambda w: (w, 0, 0, 0, 0, 0)),
        out_shape=jax.ShapeDtypeStruct((waves, groups, share, fields, cap, width), BF16),
        compiler_params=params(60),
        cost_estimate=cost(40 * x.size, 6 * x.size + 2 * a.size),
        name="diffuse",
    )(x, a)


def turn(x, count, inverse):
    rest = x - count * jnp.floor(x * inverse)
    quarters = rest * (4.0 * inverse)
    near = jnp.floor(quarters + 0.5)
    angle = (quarters - near) * 1.5707963267948966
    square = angle * angle
    sine = angle * (
        1.0 + square * (-1.0 / 6 + square * (1.0 / 120 + square * (-1.0 / 5040 + square / 362880)))
    )
    cosine = 1.0 + square * (
        -0.5 + square * (1.0 / 24 + square * (-1.0 / 720 + square / 40320))
    )
    which = near.astype(jnp.int32) & 3
    odd = (which & 1) == 1
    cos_abs = jnp.where(odd, sine, cosine)
    sin_abs = jnp.where(odd, cosine, sine)
    cos_value = jnp.where((which == 1) | (which == 2), -cos_abs, cos_abs)
    sin_value = jnp.where(which >= 2, -sin_abs, sin_abs)
    return cos_value, sin_value


def table_kernel(chunks, count_ref, inverse_ref, scale_ref, m_ref, *refs):
    group = refs[0].shape[1]
    coarse_ref = refs[-1]
    step = lax.broadcasted_iota(jnp.int32, (ROWS, LANE), 0).astype(F32)
    spots = [(c, g) for c, size in enumerate(chunks) for g in range(size)]

    def one(i, carry):
        pair = pl.program_id(0) * group + i
        count, inverse, scale = count_ref[pair], inverse_ref[pair], scale_ref[pair]
        for at, (c, g) in enumerate(spots):
            t_ref, w_ref = refs[2 * c], refs[2 * c + 1]
            base = step * m_ref[at]
            fine_cos, fine_sin = turn(base, count, inverse)
            coarse_cos, coarse_sin = turn(base * 16.0, count, inverse)
            outer_cos, outer_sin = turn(base * float(TILE), count, inverse)
            w_ref[g, i, 0:ROWS, :] = outer_cos * scale
            w_ref[g, i, ROWS : 2 * ROWS, :] = outer_sin * scale
            coarse_ref[at, 0:ROWS, :] = coarse_cos
            coarse_ref[at, ROWS : 2 * ROWS, :] = coarse_sin
            for a in range(TILE // ROWS):
                u_cos = coarse_ref[at, pl.ds(a, 1), :]
                u_sin = coarse_ref[at, pl.ds(ROWS + a, 1), :]
                rows = pl.ds(a * ROWS, ROWS)
                t_ref[g, i, rows, 0:LANE] = (u_cos * fine_cos - u_sin * fine_sin).astype(BF16)
                t_ref[g, i, rows, LANE : 2 * LANE] = (-(u_sin * fine_cos + u_cos * fine_sin)).astype(BF16)
        return carry

    lax.fori_loop(0, group, one, 0)


def phase_tables(local_pairs, m_lanes, chunks):
    pairs = local_pairs.shape[0]
    groups = m_lanes.shape[0]
    group = group_of(pairs)
    count = (4 * local_pairs + 20).astype(F32)
    specs, shapes = [], []
    for ng in chunks:
        specs.append(pl.BlockSpec((ng, group, TILE, 2 * LANE), lambda p, *_: (0, p, 0, 0)))
        specs.append(pl.BlockSpec((ng, group, 2 * ROWS, LANE), lambda p, *_: (0, p, 0, 0)))
        shapes.append(pltpu.HBM((ng, pairs, TILE, 2 * LANE), BF16))
        shapes.append(pltpu.HBM((ng, pairs, 2 * ROWS, LANE), F32))
    return pl.pallas_call(
        functools.partial(table_kernel, chunks),
        grid_spec=pltpu.PrefetchScalarGridSpec(
            num_scalar_prefetch=3,
            grid=(pairs // group,),
            in_specs=[pl.BlockSpec((groups, 1, LANE), lambda p, *_: (0, 0, 0))],
            out_specs=specs,
            scratch_shapes=[pltpu.VMEM((groups, 2 * ROWS, LANE), F32)],
        ),
        out_shape=shapes,
        compiler_params=params(48),
        cost_estimate=cost(10 * groups * pairs * TILE * 2 * LANE, 2 * groups * pairs * TILE * 2 * LANE),
        name="tables",
    )(count, 1.0 / count, 1.0 / jnp.sqrt(count), m_lanes)


def place_tiles(blocks, group, slot_ref, room_ref, x_ref, o_ref, s_ref):
    sources, share, fields, cap, width = x_ref.shape

    def unpack(source, carry):
        for l in range(share):
            for f in range(fields):
                value = x_ref[source, l, f].astype(F32)
                for h in range(2):
                    for t in range(TILE // LANE):
                        start = h * TILE + t * LANE
                        first = source * (cap * SPAN) + (h * 8 + f * share + l)
                        s_ref[t, pl.ds(first, cap, stride=SPAN), :] = value[:, start : start + LANE]
        return carry

    lax.fori_loop(0, sources, unpack, 0)
    lane = lax.broadcasted_iota(jnp.int32, (ROWS, LANE), 1)

    seen = 0
    for k, count in enumerate(blocks):

        def place(step, carry, seen=seen):
            for i in range(group):
                local = step * group + i
                first, room = slot_ref[seen + local] * SPAN, room_ref[seen + local]
                rows = pl.ds(pl.multiple_of((seen + local) * ROWS, ROWS), ROWS)
                for t in range(TILE // LANE):
                    value = s_ref[t, pl.ds(first, ROWS), :]
                    value = jnp.where(lane < room - t * LANE, value, 0.0)
                    o_ref[rows, t * LANE : (t + 1) * LANE] = value.astype(BF16)
            return carry

        lax.fori_loop(0, count, place, 0)
        seen += count * group


def rows_stage(blocks, lf, waves, pairs, stage, x_ref, t_ref, w_ref, o_ref, f_ref):
    many, group = t_ref.shape[:2]
    order = row_order(lf)
    cgs = -(-len(order) // waves)

    def pack(start, g, carry):
        for cg in range(cgs):
            items = []
            for p in range(cg * waves, (cg + 1) * waves):
                if p < len(order):
                    kind, row = order[p]
                    top = (kind * 2 * lf + row) * (group + 1)
                    items.append(f_ref[g, top : top + group, :])
                else:
                    items.append(jnp.zeros((group, LANE), F32))
            lane = pl.multiple_of((g * cgs + cg) * LANE, LANE)
            for d, value in enumerate(swap_blocks(items, LANE // waves)):
                top = d * pairs + start
                o_ref[top : top + group, pl.ds(lane, LANE)] = value.astype(BF16)
        return carry

    base = 0
    for k, count in enumerate(blocks):

        def bucket(base=base, count=count, k=k):
            def one(g, carry):
                for i in range(group):
                    rows = pl.ds((base + i * count) * ROWS, count * ROWS)
                    y = jnp.dot(x_ref[rows, :], t_ref[g, i], preferred_element_type=F32)
                    re = im = None
                    for b in range(count):
                        y_re = y[b * ROWS : (b + 1) * ROWS, 0:LANE]
                        y_im = y[b * ROWS : (b + 1) * ROWS, LANE : 2 * LANE]
                        w_cos = w_ref[g, i, b : b + 1, :]
                        w_sin = w_ref[g, i, ROWS + b : ROWS + b + 1, :]
                        add_re = w_cos * y_re + w_sin * y_im
                        add_im = w_cos * y_im - w_sin * y_re
                        re = add_re if re is None else re + add_re
                        im = add_im if im is None else im + add_im
                    for a, part in enumerate((re, im)):
                        part = part.astype(BF16).astype(F32)
                        north, south = part[0:8], part[8:16]
                        for s, total in enumerate((north + south, north - south)):
                            start = (s * 2 * lf + a * lf) * (group + 1) + i
                            f_ref[g, pl.ds(start, lf, stride=group + 1), :] = total[0:lf]
                return carry

            lax.fori_loop(0, many, one, 0)
            lax.fori_loop(0, many, functools.partial(pack, k * group), 0)

        pl.when(stage == k)(bucket)
        base += count * group

def rows_kernel(blocks, lf, waves, pairs, k_ref, t_ref, w_ref, o_ref, f_ref, x_ref, sems):
    step = pl.program_id(0)
    group = pairs // len(blocks)
    copies = []
    base = 0
    for k, count in enumerate(blocks):
        rows = pl.ds(base * ROWS, count * group * ROWS)
        copies.append(pltpu.make_async_copy(k_ref.at[rows], x_ref.at[rows], sems.at[k]))
        base += count * group

    def begin():
        for copy in copies:
            copy.start()

    pl.when(step == 0)(begin)
    for k, copy in enumerate(copies):
        pl.when(step == k)(copy.wait)
    rows_stage(blocks, lf, waves, pairs, step, x_ref, t_ref, w_ref, o_ref, f_ref)


def first_kernel(
    blocks, lf, waves, pairs, slot_ref, room_ref, a_ref, ahead_ref, t_ref, w_ref, o_ref, k_ref,
    f_ref, s_ref, x_ref, sem
):
    del ahead_ref
    step = pl.program_id(0)
    group = pairs // len(blocks)
    keep = pltpu.make_async_copy(x_ref, k_ref, sem)

    def begin():
        place_tiles(blocks, group, slot_ref, room_ref, a_ref, x_ref, s_ref)
        keep.start()

    pl.when(step == 0)(begin)
    rows_stage(blocks, lf, waves, pairs, step - 1, x_ref, t_ref, w_ref, o_ref, f_ref)
    pl.when(step == len(blocks))(keep.wait)


def table_specs(table, blocks, lag):
    ng, pairs, rows, lanes = table.shape
    at = lambda k, *_: (0, jnp.maximum(k - lag, 0), 0, 0)
    group = pairs // len(blocks)
    return [
        pl.BlockSpec((ng, group, rows, lanes), at),
        pl.BlockSpec((ng, group, 2 * ROWS, LANE), at),
    ]


def rows_cost(blocks, table, twist):
    ng, pairs, rows, lanes = table.shape
    taps = sum(blocks) * (pairs // len(blocks)) * ROWS * rows
    return cost(ng * 2 * taps * lanes, 2 * taps + 2 * table.size + 4 * twist.size)


def first_rows(arrived, slots, room, ahead, table, twist, blocks, lf, waves):
    sources, share, fields, cap, width = arrived.shape
    ng, pairs = table.shape[:2]
    cgs = -(-4 * lf // waves)
    return pl.pallas_call(
        functools.partial(first_kernel, blocks, lf, waves, pairs),
        grid_spec=pltpu.PrefetchScalarGridSpec(
            num_scalar_prefetch=2,
            grid=(len(blocks) + 1,),
            in_specs=[
                pl.BlockSpec(memory_space=pltpu.VMEM),
                pl.BlockSpec(memory_space=pl.ANY),
            ]
            + table_specs(table, blocks, 1),
            out_specs=[
                pl.BlockSpec((waves * pairs, ng * cgs * LANE), lambda k, *_: (0, 0)),
                pl.BlockSpec(memory_space=pl.ANY),
            ],
            scratch_shapes=[
                pltpu.VMEM((ng, 4 * lf * (pairs // len(blocks) + 1), LANE), F32),
                pltpu.VMEM((TILE // LANE, sources * cap * SPAN, LANE), F32),
                pltpu.VMEM((slots.shape[0] * ROWS, TILE), BF16),
                pltpu.SemaphoreType.DMA,
            ],
        ),
        out_shape=[
            pltpu.HBM((waves * pairs, ng * cgs * LANE), BF16),
            pltpu.HBM((slots.shape[0] * ROWS, TILE), BF16),
        ],
        compiler_params=params(57),
        cost_estimate=rows_cost(blocks, table, twist),
        name="place_and_rows",
    )(slots, room, arrived, ahead, table, twist)


def rows_to_waves(tiles, table, twist, blocks, lf, waves):
    ng, pairs = table.shape[:2]
    cgs = -(-4 * lf // waves)
    return pl.pallas_call(
        functools.partial(rows_kernel, blocks, lf, waves, pairs),
        grid=(len(blocks),),
        in_specs=[pl.BlockSpec(memory_space=pl.ANY)]
        + table_specs(table, blocks, 0),
        out_specs=pl.BlockSpec((waves * pairs, ng * cgs * LANE), lambda k: (0, 0)),
        out_shape=pltpu.HBM((waves * pairs, ng * cgs * LANE), BF16),
        scratch_shapes=[
            pltpu.VMEM((ng, 4 * lf * (pairs // len(blocks) + 1), LANE), F32),
            pltpu.VMEM(tiles.shape, BF16),
            pltpu.SemaphoreType.DMA((len(blocks),)),
        ],
        compiler_params=params(60),
        cost_estimate=rows_cost(blocks, table, twist),
        name="rows_to_waves",
    )(tiles, table, twist)


def legendre_kernel(g0, per_group, waves, lf, total, own_ref, r_ref, p_ref, l_ref, *rest):
    s_ref, o_ref, d_ref, b_ref = rest[-4:]
    width = LANE // waves
    span = width + 1
    group, stage = pl.program_id(0), pl.program_id(1)
    many = l_ref.shape[0]
    order = row_order(lf)
    tiles = len(order) // 8
    rows = r_ref.shape[1]
    coefs = l_ref.shape[1]
    lanes = l_ref.shape[2] // LANE

    def begin():
        value = lax.dot_general(
            r_ref[...], p_ref[...], (((0,), (0,)), ((), ())), preferred_element_type=F32
        )
        for p in range(rows // width):
            for t in range(lanes):
                d_ref[t, p * span : p * span + width, :] = value[
                    p * width : (p + 1) * width, t * LANE : (t + 1) * LANE
                ]
        if rows > len(order) * width:
            b_ref[...] = jnp.zeros_like(b_ref)

    pl.when(stage == 0)(begin)
    ordinal = lax.broadcasted_iota(jnp.int32, (8, coefs), 1)
    low_rows = lax.broadcasted_iota(jnp.int32, (8, coefs), 0) < 4

    for i in range(many):
        local = stage * many + i
        q = own_ref[(g0 + group) * per_group + local]

        def where_rows(w, tile, local=local):
            return pl.ds(tile * 8 * span + 2 * local + w, 8, stride=span)

        picked = []
        for w in range(2):
            for tile in range(tiles):
                cut = where_rows(w, tile)
                picked.append(jnp.concatenate([d_ref[t, cut, :] for t in range(lanes)], axis=1))
        left = jnp.concatenate(picked, axis=0).astype(BF16)
        forward = lax.dot_general(
            left, l_ref[i], (((1,), (1,)), ((), ())), preferred_element_type=F32
        )
        split = total - q
        low = ordinal < split
        even = jnp.where(low, ordinal & 1, (ordinal - split) & 1) == 0
        chosen = [
            jnp.where(low, forward[t * 8 : t * 8 + 8], forward[(tiles + t) * 8 : (tiles + t) * 8 + 8])
            for t in range(tiles)
        ]
        head = jnp.where(even, chosen[0], chosen[1])
        tail = jnp.where(even, chosen[2], pltpu.roll(chosen[2], 4, 0))
        s_ref[i, 0:8, :] = head
        s_ref[i, 8:12, :] = tail[0:4]
        degree = jnp.where(low, q + ordinal, ordinal - 1).astype(F32)
        damping = 1.0 / (1.0 + 8.0 * degree * (degree + 1.0) / (total * total))
        head = head * damping
        tail = tail * damping
        tail = jnp.where(low_rows, tail, pltpu.roll(tail, 4, 0))
        parts = [head, jnp.where(even, head, -head), jnp.where(even | low_rows, tail, -tail)]
        back = jnp.concatenate(
            [jnp.where(low, x, 0.0) for x in parts] + [jnp.where(low, 0.0, x) for x in parts], axis=0
        ).astype(BF16)
        rebuilt = jnp.dot(back, l_ref[i], preferred_element_type=F32)
        for w in range(2):
            for tile in range(tiles):
                row = (w * tiles + tile) * 8
                cut = where_rows(w, tile)
                for t in range(lanes):
                    b_ref[t, cut, :] = rebuilt[row : row + 8, t * LANE : (t + 1) * LANE]

    def end():
        lines = []
        for p in range(rows // width):
            cut = pl.ds(p * span, width)
            lines.append(jnp.concatenate([b_ref[t, cut, :] for t in range(lanes)], axis=1))
        value = jnp.concatenate(lines, axis=0).astype(BF16)
        o_ref[...] = lax.dot_general(
            p_ref[...], value, (((1,), (1,)), ((), ())), preferred_element_type=F32
        ).astype(BF16)

    pl.when(stage == pl.num_programs(1) - 1)(end)


def legendre_both(received, places, legendre, own_sets, lf, waves, chunk, spectral):
    sets, coefs, pair_total = legendre.shape
    cgs = -(-4 * lf // waves)
    rows = cgs * LANE
    per_group = LANE // waves // 2
    many = 4
    stages = per_group // many
    g0, ng = chunk
    block = lambda g, k, *_: ((g0 + g) * stages + k, 0, 0)
    in_specs = [
        pl.BlockSpec((pair_total, rows), lambda g, k, *_: (0, g)),
        pl.BlockSpec((pair_total, pair_total), lambda g, k, *_: (0, 0)),
        pl.BlockSpec((many, coefs, pair_total), block),
    ]
    operands = [own_sets, received, places, legendre]
    aliases = {}
    if spectral is not None:
        in_specs.append(pl.BlockSpec(memory_space=pl.ANY))
        operands.append(spectral)
        aliases = {4: 0}
    return pl.pallas_call(
        functools.partial(legendre_kernel, g0, per_group, waves, lf, coefs - 1),
        grid_spec=pltpu.PrefetchScalarGridSpec(
            num_scalar_prefetch=1,
            grid=(ng, stages),
            in_specs=in_specs,
            out_specs=[
                pl.BlockSpec((many, 2 * lf, coefs), block),
                pl.BlockSpec((pair_total, rows), lambda g, k, *_: (0, g)),
            ],
            scratch_shapes=[
                pltpu.VMEM((pair_total // LANE, cgs * (LANE + waves), LANE), F32),
                pltpu.VMEM((pair_total // LANE, cgs * (LANE + waves), LANE), F32),
            ],
        ),
        out_shape=[
            jax.ShapeDtypeStruct((sets, 2 * lf, coefs), F32),
            pltpu.HBM((pair_total, ng * rows), BF16),
        ],
        input_output_aliases=aliases,
        compiler_params=params(60),
        cost_estimate=cost(
            ng * per_group * 4 * 48 * coefs * pair_total, ng * per_group * 2 * coefs * pair_total
        ),
        name="legendre",
    )(*operands)


def unpack_kernel(order, lf, *refs):
    perm_ref, o_ref, g_ref = refs[-3:]
    parts = refs[:-3]
    sources, piece = parts[0].shape[0], parts[0].shape[1]
    cgs = -(-len(order) // sources)
    g = 0
    for ref in parts:
        for local in range(ref.shape[2] // (cgs * LANE)):
            for cg in range(cgs):
                start = (local * cgs + cg) * LANE
                items = [ref[s, :, start : start + LANE] for s in range(sources)]
                for d, value in enumerate(swap_blocks(items, LANE // sources)):
                    p = cg * sources + d
                    if p < len(order):
                        kind, row = order[p]
                        top = (kind * 2 * lf + row) * piece
                        g_ref[g, top : top + piece, :] = value
            g += 1
    left = jnp.concatenate([g_ref[t] for t in range(g)], axis=1)
    value = jnp.dot(left, perm_ref[...], preferred_element_type=F32).astype(BF16)
    o_ref[...] = value.reshape(o_ref.shape)


def unpack_rows(parts, perm, lf, waves):
    pairs = parts[0].shape[0] // waves
    piece = 16 if pairs % 16 == 0 else pairs
    total = perm.shape[0]
    shaped = [x.reshape(waves, pairs, x.shape[1]) for x in parts]
    size = sum(x.size for x in shaped)
    return pl.pallas_call(
        functools.partial(unpack_kernel, row_order(lf), lf),
        grid=(pairs // piece,),
        in_specs=[pl.BlockSpec((waves, piece, x.shape[2]), lambda j: (0, j, 0)) for x in shaped]
        + [
            pl.BlockSpec((total, total), lambda j: (0, 0)),
        ],
        out_specs=pl.BlockSpec((4 * lf, piece, total), lambda j: (0, j, 0)),
        out_shape=jax.ShapeDtypeStruct((4 * lf, pairs, total), BF16),
        scratch_shapes=[pltpu.VMEM((total // LANE, piece * 4 * lf, LANE), BF16)],
        compiler_params=params(32),
        cost_estimate=cost(2 * size * total, 4 * size),
        name="unpack",
    )(*shaped, perm)


def body(grid_fields, diffusivity, tile_map, pair_order, m_order, legendre):
    waves = lax.axis_size("wave")
    groups = lax.axis_size("lev")
    me = lax.axis_index("wave")
    levels, fields, slots, width = grid_fields.shape
    cap = slots // waves
    share = levels // groups
    lf = share * fields
    pair_total = pair_order.shape[0]
    pairs = pair_total // waves
    set_total = m_order.shape[0]
    sets = set_total // waves
    waves_total = 2 * set_total
    lane_groups = waves_total // LANE
    run = LANE // waves

    outgoing = diffuse(grid_fields, diffusivity, waves, groups)
    outgoing = outgoing.reshape(waves * groups, share, fields, cap, width)
    arrived = lax.all_to_all(outgoing, ("wave", "lev"), 0, 0, tiled=True)

    local_pairs = lax.dynamic_slice_in_dim(pair_order, me * pairs, pairs)
    picks = jnp.stack([m_order, waves_total - 1 - m_order], axis=1)
    m_lanes = picks.reshape(waves, lane_groups, run).transpose(1, 0, 2)
    m_lanes = m_lanes.reshape(lane_groups, 1, LANE).astype(F32)
    chunks = CHUNKS if sum(CHUNKS) == lane_groups else (lane_groups,)
    tables = phase_tables(local_pairs, m_lanes, chunks)

    group = group_of(pairs)
    stages = pairs // group
    blocks = []
    for k in range(stages):
        largest = waves * (k * group + group - 1) + waves - 1
        blocks.append(min(BLK, -(-(4 * largest + 20) // TILE)))
    pair_at = [k * group + i for k in range(stages) for i in range(group) for _ in range(blocks[k])]
    block_at = [b for k in range(stages) for i in range(group) for b in range(blocks[k])]
    pair_at = jnp.asarray(pair_at, jnp.int32)
    block_at = jnp.asarray(block_at, jnp.int32)
    pair_ids = jnp.take(local_pairs, pair_at)
    wanted = pair_ids * BLK + block_at
    room = 4 * pair_ids + 20 - block_at * TILE
    catalog = tile_map.reshape(waves, groups, waves, cap)
    own = lax.dynamic_index_in_dim(catalog, me, axis=2, keepdims=False).reshape(-1)
    slot_ids = jnp.arange(own.shape[0], dtype=jnp.int32)
    found = jnp.where(own[None, :] == wanted[:, None], slot_ids[None, :], 0)
    slot_of = jnp.max(found, axis=1)

    places = (pair_order[:, None] == jnp.arange(pair_total, dtype=jnp.int32)[None, :]).astype(BF16)
    own_sets = lax.dynamic_slice_in_dim(m_order, me * sets, sets)
    lane = jnp.arange(waves_total, dtype=jnp.int32)
    spot = lane // LANE * run + lane % run
    column = spot % 2 * set_total + lane % LANE // run * sets + spot // 2
    perm = (column[:, None] == lane[None, :]).astype(BF16)

    received = []
    for c in range(len(chunks)):
        pieces = tables[2 * c], tables[2 * c + 1], tuple(blocks), lf, waves
        if c == 0:
            sent, tiles = first_rows(arrived, slot_of, room, legendre, *pieces)
        else:
            sent = rows_to_waves(tiles, *pieces)
        received.append(lax.all_to_all(sent, "wave", 0, 0, tiled=True))
    spectral = None
    returned = []
    begin = 0
    for ng, part in zip(chunks, received):
        spectral, back = legendre_both(
            part, places, legendre, own_sets, lf, waves, (begin, ng), spectral
        )
        begin += ng
        returned.append(lax.all_to_all(back, "wave", 0, 0, tiled=True))
    fourier_out = unpack_rows(returned, perm, lf, waves)
    spectral = spectral.reshape(sets, 2, fields, share, legendre.shape[1])
    fourier_out = fourier_out.transpose(1, 0, 2).reshape(pairs, 2, 2, fields, share, waves_total)
    return spectral, fourier_out


def solution(mesh):
    return jax.shard_map(
        body,
        mesh=mesh,
        in_specs=(
            P(None, None, ("wave", "lev"), None),
            P(None, ("wave", "lev"), None),
            P(),
            P(),
            P(),
            P("wave", None, None),
        ),
        out_specs=(P("wave", None, None, "lev", None), P("wave", None, None, None, "lev", None)),
        check_vma=False,
    )
```

```python
import functools

import jax
import jax.numpy as jnp
from jax import lax
from jax.experimental import pallas as pl
from jax.experimental.pallas import tpu as pltpu
from jax.sharding import PartitionSpec as P

TILE = 256
BLK = 11
SPAN = 17
LANE = 128
ROWS = 16
F32 = jnp.float32
BF16 = jnp.bfloat16
MIB = 1024 * 1024
CHUNKS = (2, 3)
OWNERS = 4


def group_of(pairs):
    return 16 if pairs % 16 == 0 else 8


def params(mib):
    return pltpu.CompilerParams(vmem_limit_bytes=mib * MIB)


def cost(flops, moved):
    return pl.CostEstimate(flops=int(flops), bytes_accessed=int(moved), transcendentals=0)


def row_order(lf):
    full = 2 * lf
    head = full // 8 * 8
    rows = []
    for start in range(0, head, 8):
        for kind in range(2):
            rows += [(kind, start + i) for i in range(8)]
    rest = full - head
    assert 2 * rest == 8 and head == 8
    for kind in range(2):
        rows += [(kind, head + i) for i in range(rest)]
    return rows


def swap_blocks(items, width):
    items = list(items)
    lane = lax.broadcasted_iota(jnp.int32, items[0].shape, 1)
    step = 1
    while step < len(items):
        reach = width * step
        low = (lane & reach) == 0
        for i in range(len(items)):
            if i & step:
                continue
            first, second = items[i], items[i + step]
            items[i] = jnp.where(low, first, pltpu.roll(second, reach, 1))
            items[i + step] = jnp.where(low, pltpu.roll(first, LANE - reach, 1), second)
        step *= 2
    return items


def diffuse_kernel(share, x_ref, a_ref, o_ref):
    levels, fields = x_ref.shape[0], x_ref.shape[1]
    width = x_ref.shape[-1]
    for w, start in [(w, start) for w in range(x_ref.shape[2]) for start in range(0, width, LANE)]:
        cut = pl.ds(start, LANE)
        coef = [a_ref[k, w, :, cut].astype(F32) for k in range(levels - 1)]
        ratios = []
        partials = [[] for _ in range(fields)]
        for k in range(levels):
            if k == 0:
                pivot = 1.0 + coef[0]
            elif k == levels - 1:
                pivot = 1.0 + coef[k - 1] - coef[k - 1] * ratios[k - 1]
            else:
                pivot = 1.0 + coef[k - 1] + coef[k] - coef[k - 1] * ratios[k - 1]
            inverse = 1.0 / pivot
            if k < levels - 1:
                ratios.append(coef[k] * inverse)
            for f in range(fields):
                value = x_ref[k, f, w, :, cut]
                if k:
                    value = value + coef[k - 1] * partials[f][k - 1]
                partials[f].append(value * inverse)
        for f in range(fields):
            solved = None
            for k in range(levels - 1, -1, -1):
                solved = partials[f][k] if solved is None else partials[f][k] + ratios[k] * solved
                o_ref[w, k // share, k % share, f, :, cut] = solved.astype(BF16)


def diffuse(grid_fields, diffusivity, waves, groups):
    levels, fields, slots, width = grid_fields.shape
    cap = slots // waves
    share = levels // groups
    x = grid_fields.reshape(levels, fields, waves, cap, width)
    a = diffusivity.reshape(levels - 1, waves, cap, width)
    return pl.pallas_call(
        functools.partial(diffuse_kernel, share),
        grid=(waves // OWNERS,),
        in_specs=[
            pl.BlockSpec((levels, fields, OWNERS, cap, width), lambda w: (0, 0, w, 0, 0)),
            pl.BlockSpec((levels - 1, OWNERS, cap, width), lambda w: (0, w, 0, 0)),
        ],
        out_specs=pl.BlockSpec((OWNERS, groups, share, fields, cap, width), lambda w: (w, 0, 0, 0, 0, 0)),
        out_shape=jax.ShapeDtypeStruct((waves, groups, share, fields, cap, width), BF16),
        compiler_params=params(60),
        cost_estimate=cost(40 * x.size, 6 * x.size + 2 * a.size),
        name="diffuse",
    )(x, a)


def turn(x, count, inverse):
    rest = x - count * jnp.floor(x * inverse)
    quarters = rest * (4.0 * inverse)
    near = jnp.floor(quarters + 0.5)
    angle = (quarters - near) * 1.5707963267948966
    square = angle * angle
    sine = angle * (
        1.0 + square * (-1.0 / 6 + square * (1.0 / 120 + square * (-1.0 / 5040 + square / 362880)))
    )
    cosine = 1.0 + square * (
        -0.5 + square * (1.0 / 24 + square * (-1.0 / 720 + square / 40320))
    )
    which = near.astype(jnp.int32) & 3
    odd = (which & 1) == 1
    cos_abs = jnp.where(odd, sine, cosine)
    sin_abs = jnp.where(odd, cosine, sine)
    cos_value = jnp.where((which == 1) | (which == 2), -cos_abs, cos_abs)
    sin_value = jnp.where(which >= 2, -sin_abs, sin_abs)
    return cos_value, sin_value


def table_kernel(chunks, count_ref, inverse_ref, scale_ref, m_ref, *refs):
    group = refs[0].shape[1]
    coarse_ref = refs[-1]
    step = lax.broadcasted_iota(jnp.int32, (ROWS, LANE), 0).astype(F32)
    spots = [(c, g) for c, size in enumerate(chunks) for g in range(size)]

    def one(i, carry):
        pair = pl.program_id(0) * group + i
        count, inverse, scale = count_ref[pair], inverse_ref[pair], scale_ref[pair]
        for at, (c, g) in enumerate(spots):
            t_ref, w_ref = refs[2 * c], refs[2 * c + 1]
            base = step * m_ref[at]
            fine_cos, fine_sin = turn(base, count, inverse)
            coarse_cos, coarse_sin = turn(base * 16.0, count, inverse)
            outer_cos, outer_sin = turn(base * float(TILE), count, inverse)
            w_ref[g, i, 0:ROWS, :] = outer_cos * scale
            w_ref[g, i, ROWS : 2 * ROWS, :] = outer_sin * scale
            coarse_ref[at, 0:ROWS, :] = coarse_cos
            coarse_ref[at, ROWS : 2 * ROWS, :] = coarse_sin
            for a in range(TILE // ROWS):
                u_cos = coarse_ref[at, pl.ds(a, 1), :]
                u_sin = coarse_ref[at, pl.ds(ROWS + a, 1), :]
                rows = pl.ds(a * ROWS, ROWS)
                t_ref[g, i, rows, 0:LANE] = (u_cos * fine_cos - u_sin * fine_sin).astype(BF16)
                t_ref[g, i, rows, LANE : 2 * LANE] = (-(u_sin * fine_cos + u_cos * fine_sin)).astype(BF16)
        return carry

    lax.fori_loop(0, group, one, 0)


def phase_tables(local_pairs, m_lanes, chunks):
    pairs = local_pairs.shape[0]
    groups = m_lanes.shape[0]
    group = group_of(pairs)
    count = (4 * local_pairs + 20).astype(F32)
    specs, shapes = [], []
    for ng in chunks:
        specs.append(pl.BlockSpec((ng, group, TILE, 2 * LANE), lambda p, *_: (0, p, 0, 0)))
        specs.append(pl.BlockSpec((ng, group, 2 * ROWS, LANE), lambda p, *_: (0, p, 0, 0)))
        shapes.append(pltpu.HBM((ng, pairs, TILE, 2 * LANE), BF16))
        shapes.append(pltpu.HBM((ng, pairs, 2 * ROWS, LANE), F32))
    return pl.pallas_call(
        functools.partial(table_kernel, chunks),
        grid_spec=pltpu.PrefetchScalarGridSpec(
            num_scalar_prefetch=3,
            grid=(pairs // group,),
            in_specs=[pl.BlockSpec((groups, 1, LANE), lambda p, *_: (0, 0, 0))],
            out_specs=specs,
            scratch_shapes=[pltpu.VMEM((groups, 2 * ROWS, LANE), F32)],
        ),
        out_shape=shapes,
        compiler_params=params(48),
        cost_estimate=cost(10 * groups * pairs * TILE * 2 * LANE, 2 * groups * pairs * TILE * 2 * LANE),
        name="tables",
    )(count, 1.0 / count, 1.0 / jnp.sqrt(count), m_lanes)


def place_tiles(blocks, group, slot_ref, room_ref, x_ref, o_ref, s_ref):
    sources, share, fields, cap, width = x_ref.shape

    def unpack(source, carry):
        for l in range(share):
            for f in range(fields):
                value = x_ref[source, l, f].astype(F32)
                for h in range(2):
                    for t in range(TILE // LANE):
                        start = h * TILE + t * LANE
                        first = source * (cap * SPAN) + (h * 8 + f * share + l)
                        s_ref[t, pl.ds(first, cap, stride=SPAN), :] = value[:, start : start + LANE]
        return carry

    lax.fori_loop(0, sources, unpack, 0)
    lane = lax.broadcasted_iota(jnp.int32, (ROWS, LANE), 1)

    seen = 0
    for k, count in enumerate(blocks):

        def place(step, carry, seen=seen):
            for i in range(group):
                local = step * group + i
                first, room = slot_ref[seen + local] * SPAN, room_ref[seen + local]
                rows = pl.ds(pl.multiple_of((seen + local) * ROWS, ROWS), ROWS)
                for t in range(TILE // LANE):
                    value = s_ref[t, pl.ds(first, ROWS), :]
                    value = jnp.where(lane < room - t * LANE, value, 0.0)
                    o_ref[rows, t * LANE : (t + 1) * LANE] = value.astype(BF16)
            return carry

        lax.fori_loop(0, count, place, 0)
        seen += count * group


def rows_stage(blocks, lf, waves, pairs, stage, x_ref, t_ref, w_ref, o_ref, f_ref):
    many, group = t_ref.shape[:2]
    order = row_order(lf)
    cgs = -(-len(order) // waves)

    def pack(start, g, carry):
        for cg in range(cgs):
            items = []
            for p in range(cg * waves, (cg + 1) * waves):
                if p < len(order):
                    kind, row = order[p]
                    top = (kind * 2 * lf + row) * (group + 1)
                    items.append(f_ref[g, top : top + group, :])
                else:
                    items.append(jnp.zeros((group, LANE), F32))
            lane = pl.multiple_of((g * cgs + cg) * LANE, LANE)
            for d, value in enumerate(swap_blocks(items, LANE // waves)):
                top = d * pairs + start
                o_ref[top : top + group, pl.ds(lane, LANE)] = value.astype(BF16)
        return carry

    base = 0
    for k, count in enumerate(blocks):

        def bucket(base=base, count=count, k=k):
            def one(g, carry):
                for i in range(group):
                    rows = pl.ds((base + i * count) * ROWS, count * ROWS)
                    y = jnp.dot(x_ref[rows, :], t_ref[g, i], preferred_element_type=F32)
                    re = im = None
                    for b in range(count):
                        y_re = y[b * ROWS : (b + 1) * ROWS, 0:LANE]
                        y_im = y[b * ROWS : (b + 1) * ROWS, LANE : 2 * LANE]
                        w_cos = w_ref[g, i, b : b + 1, :]
                        w_sin = w_ref[g, i, ROWS + b : ROWS + b + 1, :]
                        add_re = w_cos * y_re + w_sin * y_im
                        add_im = w_cos * y_im - w_sin * y_re
                        re = add_re if re is None else re + add_re
                        im = add_im if im is None else im + add_im
                    for a, part in enumerate((re, im)):
                        part = part.astype(BF16).astype(F32)
                        north, south = part[0:8], part[8:16]
                        for s, total in enumerate((north + south, north - south)):
                            start = (s * 2 * lf + a * lf) * (group + 1) + i
                            f_ref[g, pl.ds(start, lf, stride=group + 1), :] = total[0:lf]
                return carry

            lax.fori_loop(0, many, one, 0)
            lax.fori_loop(0, many, functools.partial(pack, k * group), 0)

        pl.when(stage == k)(bucket)
        base += count * group

def rows_kernel(blocks, lf, waves, pairs, k_ref, t_ref, w_ref, o_ref, f_ref, x_ref, sems):
    step = pl.program_id(0)
    group = pairs // len(blocks)
    copies = []
    base = 0
    for k, count in enumerate(blocks):
        rows = pl.ds(base * ROWS, count * group * ROWS)
        copies.append(pltpu.make_async_copy(k_ref.at[rows], x_ref.at[rows], sems.at[k]))
        base += count * group

    def begin():
        for copy in copies:
            copy.start()

    pl.when(step == 0)(begin)
    for k, copy in enumerate(copies):
        pl.when(step == k)(copy.wait)
    rows_stage(blocks, lf, waves, pairs, step, x_ref, t_ref, w_ref, o_ref, f_ref)


def first_kernel(
    blocks, lf, waves, pairs, slot_ref, room_ref, a_ref, ahead_ref, t_ref, w_ref, o_ref, k_ref,
    f_ref, s_ref, x_ref, sem
):
    del ahead_ref
    step = pl.program_id(0)
    group = pairs // len(blocks)
    keep = pltpu.make_async_copy(x_ref, k_ref, sem)

    def begin():
        place_tiles(blocks, group, slot_ref, room_ref, a_ref, x_ref, s_ref)
        keep.start()

    pl.when(step == 0)(begin)
    rows_stage(blocks, lf, waves, pairs, step - 1, x_ref, t_ref, w_ref, o_ref, f_ref)
    pl.when(step == len(blocks))(keep.wait)


def table_specs(table, blocks, lag):
    ng, pairs, rows, lanes = table.shape
    at = lambda k, *_: (0, jnp.maximum(k - lag, 0), 0, 0)
    group = pairs // len(blocks)
    return [
        pl.BlockSpec((ng, group, rows, lanes), at),
        pl.BlockSpec((ng, group, 2 * ROWS, LANE), at),
    ]


def rows_cost(blocks, table, twist):
    ng, pairs, rows, lanes = table.shape
    taps = sum(blocks) * (pairs // len(blocks)) * ROWS * rows
    return cost(ng * 2 * taps * lanes, 2 * taps + 2 * table.size + 4 * twist.size)


def first_rows(arrived, slots, room, ahead, table, twist, blocks, lf, waves):
    sources, share, fields, cap, width = arrived.shape
    ng, pairs = table.shape[:2]
    cgs = -(-4 * lf // waves)
    return pl.pallas_call(
        functools.partial(first_kernel, blocks, lf, waves, pairs),
        grid_spec=pltpu.PrefetchScalarGridSpec(
            num_scalar_prefetch=2,
            grid=(len(blocks) + 1,),
            in_specs=[
                pl.BlockSpec(memory_space=pltpu.VMEM),
                pl.BlockSpec(memory_space=pl.ANY),
            ]
            + table_specs(table, blocks, 1),
            out_specs=[
                pl.BlockSpec((waves * pairs, ng * cgs * LANE), lambda k, *_: (0, 0)),
                pl.BlockSpec(memory_space=pl.ANY),
            ],
            scratch_shapes=[
                pltpu.VMEM((ng, 4 * lf * (pairs // len(blocks) + 1), LANE), F32),
                pltpu.VMEM((TILE // LANE, sources * cap * SPAN, LANE), F32),
                pltpu.VMEM((slots.shape[0] * ROWS, TILE), BF16),
                pltpu.SemaphoreType.DMA,
            ],
        ),
        out_shape=[
            pltpu.HBM((waves * pairs, ng * cgs * LANE), BF16),
            pltpu.HBM((slots.shape[0] * ROWS, TILE), BF16),
        ],
        compiler_params=params(48),
        cost_estimate=rows_cost(blocks, table, twist),
        name="place_and_rows",
    )(slots, room, arrived, ahead, table, twist)


def rows_to_waves(tiles, table, twist, blocks, lf, waves):
    ng, pairs = table.shape[:2]
    cgs = -(-4 * lf // waves)
    return pl.pallas_call(
        functools.partial(rows_kernel, blocks, lf, waves, pairs),
        grid=(len(blocks),),
        in_specs=[pl.BlockSpec(memory_space=pl.ANY)]
        + table_specs(table, blocks, 0),
        out_specs=pl.BlockSpec((waves * pairs, ng * cgs * LANE), lambda k: (0, 0)),
        out_shape=pltpu.HBM((waves * pairs, ng * cgs * LANE), BF16),
        scratch_shapes=[
            pltpu.VMEM((ng, 4 * lf * (pairs // len(blocks) + 1), LANE), F32),
            pltpu.VMEM(tiles.shape, BF16),
            pltpu.SemaphoreType.DMA((len(blocks),)),
        ],
        compiler_params=params(60),
        cost_estimate=rows_cost(blocks, table, twist),
        name="rows_to_waves",
    )(tiles, table, twist)


def legendre_kernel(g0, per_group, waves, lf, total, own_ref, r_ref, p_ref, l_ref, *rest):
    s_ref, o_ref, d_ref, b_ref = rest[-4:]
    width = LANE // waves
    span = width + 1
    group, stage = pl.program_id(0), pl.program_id(1)
    many = l_ref.shape[0]
    order = row_order(lf)
    tiles = len(order) // 8
    rows = r_ref.shape[1]
    coefs = l_ref.shape[1]
    lanes = l_ref.shape[2] // LANE

    def begin():
        value = lax.dot_general(
            r_ref[...], p_ref[...], (((0,), (0,)), ((), ())), preferred_element_type=F32
        )
        for p in range(rows // width):
            for t in range(lanes):
                d_ref[t, p * span : p * span + width, :] = value[
                    p * width : (p + 1) * width, t * LANE : (t + 1) * LANE
                ]
        if rows > len(order) * width:
            b_ref[...] = jnp.zeros_like(b_ref)

    pl.when(stage == 0)(begin)
    ordinal = lax.broadcasted_iota(jnp.int32, (8, coefs), 1)
    low_rows = lax.broadcasted_iota(jnp.int32, (8, coefs), 0) < 4

    for i in range(many):
        local = stage * many + i
        q = own_ref[(g0 + group) * per_group + local]

        def where_rows(w, tile, local=local):
            return pl.ds(tile * 8 * span + 2 * local + w, 8, stride=span)

        picked = []
        for w in range(2):
            for tile in range(tiles):
                cut = where_rows(w, tile)
                picked.append(jnp.concatenate([d_ref[t, cut, :] for t in range(lanes)], axis=1))
        left = jnp.concatenate(picked, axis=0).astype(BF16)
        forward = lax.dot_general(
            left, l_ref[i], (((1,), (1,)), ((), ())), preferred_element_type=F32
        )
        split = total - q
        low = ordinal < split
        even = jnp.where(low, ordinal & 1, (ordinal - split) & 1) == 0
        chosen = [
            jnp.where(low, forward[t * 8 : t * 8 + 8], forward[(tiles + t) * 8 : (tiles + t) * 8 + 8])
            for t in range(tiles)
        ]
        head = jnp.where(even, chosen[0], chosen[1])
        tail = jnp.where(even, chosen[2], pltpu.roll(chosen[2], 4, 0))
        s_ref[i, 0:8, :] = head
        s_ref[i, 8:12, :] = tail[0:4]
        degree = jnp.where(low, q + ordinal, ordinal - 1).astype(F32)
        damping = 1.0 / (1.0 + 8.0 * degree * (degree + 1.0) / (total * total))
        head = head * damping
        tail = tail * damping
        tail = jnp.where(low_rows, tail, pltpu.roll(tail, 4, 0))
        parts = [head, jnp.where(even, head, -head), jnp.where(even | low_rows, tail, -tail)]
        back = jnp.concatenate(
            [jnp.where(low, x, 0.0) for x in parts] + [jnp.where(low, 0.0, x) for x in parts], axis=0
        ).astype(BF16)
        rebuilt = jnp.dot(back, l_ref[i], preferred_element_type=F32)
        for w in range(2):
            for tile in range(tiles):
                row = (w * tiles + tile) * 8
                cut = where_rows(w, tile)
                for t in range(lanes):
                    b_ref[t, cut, :] = rebuilt[row : row + 8, t * LANE : (t + 1) * LANE]

    def end():
        lines = []
        for p in range(rows // width):
            cut = pl.ds(p * span, width)
            lines.append(jnp.concatenate([b_ref[t, cut, :] for t in range(lanes)], axis=1))
        value = jnp.concatenate(lines, axis=0).astype(BF16)
        o_ref[...] = lax.dot_general(
            p_ref[...], value, (((1,), (1,)), ((), ())), preferred_element_type=F32
        ).astype(BF16)

    pl.when(stage == pl.num_programs(1) - 1)(end)


def legendre_both(received, places, legendre, own_sets, lf, waves, chunk, spectral):
    sets, coefs, pair_total = legendre.shape
    cgs = -(-4 * lf // waves)
    rows = cgs * LANE
    per_group = LANE // waves // 2
    many = 4
    stages = per_group // many
    g0, ng = chunk
    block = lambda g, k, *_: ((g0 + g) * stages + k, 0, 0)
    in_specs = [
        pl.BlockSpec((pair_total, rows), lambda g, k, *_: (0, g)),
        pl.BlockSpec((pair_total, pair_total), lambda g, k, *_: (0, 0)),
        pl.BlockSpec((many, coefs, pair_total), block),
    ]
    operands = [own_sets, received, places, legendre]
    aliases = {}
    if spectral is not None:
        in_specs.append(pl.BlockSpec(memory_space=pl.ANY))
        operands.append(spectral)
        aliases = {4: 0}
    return pl.pallas_call(
        functools.partial(legendre_kernel, g0, per_group, waves, lf, coefs - 1),
        grid_spec=pltpu.PrefetchScalarGridSpec(
            num_scalar_prefetch=1,
            grid=(ng, stages),
            in_specs=in_specs,
            out_specs=[
                pl.BlockSpec((many, 2 * lf, coefs), block),
                pl.BlockSpec((pair_total, rows), lambda g, k, *_: (0, g)),
            ],
            scratch_shapes=[
                pltpu.VMEM((pair_total // LANE, cgs * (LANE + waves), LANE), F32),
                pltpu.VMEM((pair_total // LANE, cgs * (LANE + waves), LANE), F32),
            ],
        ),
        out_shape=[
            jax.ShapeDtypeStruct((sets, 2 * lf, coefs), F32),
            pltpu.HBM((pair_total, ng * rows), BF16),
        ],
        input_output_aliases=aliases,
        compiler_params=params(60),
        cost_estimate=cost(
            ng * per_group * 4 * 48 * coefs * pair_total, ng * per_group * 2 * coefs * pair_total
        ),
        name="legendre",
    )(*operands)


def unpack_kernel(order, lf, *refs):
    perm_ref, o_ref, g_ref = refs[-3:]
    parts = refs[:-3]
    sources, piece = parts[0].shape[0], parts[0].shape[1]
    cgs = -(-len(order) // sources)
    g = 0
    for ref in parts:
        for local in range(ref.shape[2] // (cgs * LANE)):
            for cg in range(cgs):
                start = (local * cgs + cg) * LANE
                items = [ref[s, :, start : start + LANE] for s in range(sources)]
                for d, value in enumerate(swap_blocks(items, LANE // sources)):
                    p = cg * sources + d
                    if p < len(order):
                        kind, row = order[p]
                        top = (kind * 2 * lf + row) * piece
                        g_ref[g, top : top + piece, :] = value
            g += 1
    left = jnp.concatenate([g_ref[t] for t in range(g)], axis=1)
    value = jnp.dot(left, perm_ref[...], preferred_element_type=F32).astype(BF16)
    o_ref[...] = value.reshape(o_ref.shape)


def unpack_rows(parts, perm, lf, waves):
    pairs = parts[0].shape[0] // waves
    piece = 16 if pairs % 16 == 0 else pairs
    total = perm.shape[0]
    shaped = [x.reshape(waves, pairs, x.shape[1]) for x in parts]
    size = sum(x.size for x in shaped)
    return pl.pallas_call(
        functools.partial(unpack_kernel, row_order(lf), lf),
        grid=(pairs // piece,),
        in_specs=[pl.BlockSpec((waves, piece, x.shape[2]), lambda j: (0, j, 0)) for x in shaped]
        + [
            pl.BlockSpec((total, total), lambda j: (0, 0)),
        ],
        out_specs=pl.BlockSpec((4 * lf, piece, total), lambda j: (0, j, 0)),
        out_shape=jax.ShapeDtypeStruct((4 * lf, pairs, total), BF16),
        scratch_shapes=[pltpu.VMEM((total // LANE, piece * 4 * lf, LANE), BF16)],
        compiler_params=params(32),
        cost_estimate=cost(2 * size * total, 4 * size),
        name="unpack",
    )(*shaped, perm)


def body(grid_fields, diffusivity, tile_map, pair_order, m_order, legendre):
    waves = lax.axis_size("wave")
    groups = lax.axis_size("lev")
    me = lax.axis_index("wave")
    levels, fields, slots, width = grid_fields.shape
    cap = slots // waves
    share = levels // groups
    lf = share * fields
    pair_total = pair_order.shape[0]
    pairs = pair_total // waves
    set_total = m_order.shape[0]
    sets = set_total // waves
    waves_total = 2 * set_total
    lane_groups = waves_total // LANE
    run = LANE // waves

    outgoing = diffuse(grid_fields, diffusivity, waves, groups)
    outgoing = outgoing.reshape(waves * groups, share, fields, cap, width)
    arrived = lax.all_to_all(outgoing, ("wave", "lev"), 0, 0, tiled=True)

    local_pairs = lax.dynamic_slice_in_dim(pair_order, me * pairs, pairs)
    picks = jnp.stack([m_order, waves_total - 1 - m_order], axis=1)
    m_lanes = picks.reshape(waves, lane_groups, run).transpose(1, 0, 2)
    m_lanes = m_lanes.reshape(lane_groups, 1, LANE).astype(F32)
    chunks = CHUNKS if sum(CHUNKS) == lane_groups else (lane_groups,)
    tables = phase_tables(local_pairs, m_lanes, chunks)

    group = group_of(pairs)
    stages = pairs // group
    blocks = []
    for k in range(stages):
        largest = waves * (k * group + group - 1) + waves - 1
        blocks.append(min(BLK, -(-(4 * largest + 20) // TILE)))
    pair_at = [k * group + i for k in range(stages) for i in range(group) for _ in range(blocks[k])]
    block_at = [b for k in range(stages) for i in range(group) for b in range(blocks[k])]
    pair_at = jnp.asarray(pair_at, jnp.int32)
    block_at = jnp.asarray(block_at, jnp.int32)
    pair_ids = jnp.take(local_pairs, pair_at)
    wanted = pair_ids * BLK + block_at
    room = 4 * pair_ids + 20 - block_at * TILE
    catalog = tile_map.reshape(waves, groups, waves, cap)
    own = lax.dynamic_index_in_dim(catalog, me, axis=2, keepdims=False).reshape(-1)
    slot_ids = jnp.arange(own.shape[0], dtype=jnp.int32)
    found = jnp.where(own[None, :] == wanted[:, None], slot_ids[None, :], 0)
    slot_of = jnp.max(found, axis=1)

    places = (pair_order[:, None] == jnp.arange(pair_total, dtype=jnp.int32)[None, :]).astype(BF16)
    own_sets = lax.dynamic_slice_in_dim(m_order, me * sets, sets)
    lane = jnp.arange(waves_total, dtype=jnp.int32)
    spot = lane // LANE * run + lane % run
    column = spot % 2 * set_total + lane % LANE // run * sets + spot // 2
    perm = (column[:, None] == lane[None, :]).astype(BF16)

    received = []
    for c in range(len(chunks)):
        pieces = tables[2 * c], tables[2 * c + 1], tuple(blocks), lf, waves
        if c == 0:
            sent, tiles = first_rows(arrived, slot_of, room, legendre, *pieces)
        else:
            sent = rows_to_waves(tiles, *pieces)
        received.append(lax.all_to_all(sent, "wave", 0, 0, tiled=True))
    spectral = None
    returned = []
    begin = 0
    for ng, part in zip(chunks, received):
        spectral, back = legendre_both(
            part, places, legendre, own_sets, lf, waves, (begin, ng), spectral
        )
        begin += ng
        returned.append(lax.all_to_all(back, "wave", 0, 0, tiled=True))
    fourier_out = unpack_rows(returned, perm, lf, waves)
    spectral = spectral.reshape(sets, 2, fields, share, legendre.shape[1])
    fourier_out = fourier_out.transpose(1, 0, 2).reshape(pairs, 2, 2, fields, share, waves_total)
    return spectral, fourier_out


def solution(mesh):
    return jax.shard_map(
        body,
        mesh=mesh,
        in_specs=(
            P(None, None, ("wave", "lev"), None),
            P(None, ("wave", "lev"), None),
            P(),
            P(),
            P(),
            P("wave", None, None),
        ),
        out_specs=(P("wave", None, None, "lev", None), P("wave", None, None, None, "lev", None)),
        check_vma=False,
    )
```

```python
import functools

import jax
import jax.numpy as jnp
from jax import lax
from jax.experimental import pallas as pl
from jax.experimental.pallas import tpu as pltpu
from jax.sharding import PartitionSpec as P

TILE = 256
BLK = 11
SPAN = 17
LANE = 128
ROWS = 16
F32 = jnp.float32
BF16 = jnp.bfloat16
MIB = 1024 * 1024
CHUNKS = (2, 3)
OWNERS = 4


def group_of(pairs):
    return 16 if pairs % 16 == 0 else 8


def params(mib):
    return pltpu.CompilerParams(vmem_limit_bytes=mib * MIB)


def cost(flops, moved):
    return pl.CostEstimate(flops=int(flops), bytes_accessed=int(moved), transcendentals=0)


def row_order(lf):
    full = 2 * lf
    head = full // 8 * 8
    rows = []
    for start in range(0, head, 8):
        for kind in range(2):
            rows += [(kind, start + i) for i in range(8)]
    rest = full - head
    assert 2 * rest == 8 and head == 8
    for kind in range(2):
        rows += [(kind, head + i) for i in range(rest)]
    return rows


def swap_blocks(items, width):
    items = list(items)
    lane = lax.broadcasted_iota(jnp.int32, items[0].shape, 1)
    step = 1
    while step < len(items):
        reach = width * step
        low = (lane & reach) == 0
        for i in range(len(items)):
            if i & step:
                continue
            first, second = items[i], items[i + step]
            items[i] = jnp.where(low, first, pltpu.roll(second, reach, 1))
            items[i + step] = jnp.where(low, pltpu.roll(first, LANE - reach, 1), second)
        step *= 2
    return items


def diffuse_kernel(share, x_ref, a_ref, o_ref):
    levels, fields = x_ref.shape[0], x_ref.shape[1]
    width = x_ref.shape[-1]
    for w, start in [(w, start) for w in range(x_ref.shape[2]) for start in range(0, width, LANE)]:
        cut = pl.ds(start, LANE)
        coef = [a_ref[k, w, :, cut].astype(F32) for k in range(levels - 1)]
        ratios = []
        partials = [[] for _ in range(fields)]
        for k in range(levels):
            if k == 0:
                pivot = 1.0 + coef[0]
            elif k == levels - 1:
                pivot = 1.0 + coef[k - 1] - coef[k - 1] * ratios[k - 1]
            else:
                pivot = 1.0 + coef[k - 1] + coef[k] - coef[k - 1] * ratios[k - 1]
            inverse = 1.0 / pivot
            if k < levels - 1:
                ratios.append(coef[k] * inverse)
            for f in range(fields):
                value = x_ref[k, f, w, :, cut]
                if k:
                    value = value + coef[k - 1] * partials[f][k - 1]
                partials[f].append(value * inverse)
        for f in range(fields):
            solved = None
            for k in range(levels - 1, -1, -1):
                solved = partials[f][k] if solved is None else partials[f][k] + ratios[k] * solved
                o_ref[w, k // share, k % share, f, :, cut] = solved.astype(BF16)


def diffuse(grid_fields, diffusivity, waves, groups):
    levels, fields, slots, width = grid_fields.shape
    cap = slots // waves
    share = levels // groups
    x = grid_fields.reshape(levels, fields, waves, cap, width)
    a = diffusivity.reshape(levels - 1, waves, cap, width)
    return pl.pallas_call(
        functools.partial(diffuse_kernel, share),
        grid=(waves // OWNERS,),
        in_specs=[
            pl.BlockSpec((levels, fields, OWNERS, cap, width), lambda w: (0, 0, w, 0, 0)),
            pl.BlockSpec((levels - 1, OWNERS, cap, width), lambda w: (0, w, 0, 0)),
        ],
        out_specs=pl.BlockSpec((OWNERS, groups, share, fields, cap, width), lambda w: (w, 0, 0, 0, 0, 0)),
        out_shape=jax.ShapeDtypeStruct((waves, groups, share, fields, cap, width), BF16),
        compiler_params=params(60),
        cost_estimate=cost(40 * x.size, 6 * x.size + 2 * a.size),
        name="diffuse",
    )(x, a)


def turn(x, count, inverse):
    rest = x - count * jnp.floor(x * inverse)
    quarters = rest * (4.0 * inverse)
    near = jnp.floor(quarters + 0.5)
    angle = (quarters - near) * 1.5707963267948966
    square = angle * angle
    sine = angle * (
        1.0 + square * (-1.0 / 6 + square * (1.0 / 120 + square * (-1.0 / 5040 + square / 362880)))
    )
    cosine = 1.0 + square * (
        -0.5 + square * (1.0 / 24 + square * (-1.0 / 720 + square / 40320))
    )
    which = near.astype(jnp.int32) & 3
    odd = (which & 1) == 1
    cos_abs = jnp.where(odd, sine, cosine)
    sin_abs = jnp.where(odd, cosine, sine)
    cos_value = jnp.where((which == 1) | (which == 2), -cos_abs, cos_abs)
    sin_value = jnp.where(which >= 2, -sin_abs, sin_abs)
    return cos_value, sin_value


def table_kernel(chunks, count_ref, inverse_ref, scale_ref, m_ref, *refs):
    group = refs[0].shape[1]
    coarse_ref = refs[-1]
    step = lax.broadcasted_iota(jnp.int32, (ROWS, LANE), 0).astype(F32)
    spots = [(c, g) for c, size in enumerate(chunks) for g in range(size)]

    def one(i, carry):
        pair = pl.program_id(0) * group + i
        count, inverse, scale = count_ref[pair], inverse_ref[pair], scale_ref[pair]
        for at, (c, g) in enumerate(spots):
            t_ref, w_ref = refs[2 * c], refs[2 * c + 1]
            base = step * m_ref[at]
            fine_cos, fine_sin = turn(base, count, inverse)
            coarse_cos, coarse_sin = turn(base * 16.0, count, inverse)
            outer_cos, outer_sin = turn(base * float(TILE), count, inverse)
            w_ref[g, i, 0:ROWS, :] = outer_cos * scale
            w_ref[g, i, ROWS : 2 * ROWS, :] = outer_sin * scale
            coarse_ref[at, 0:ROWS, :] = coarse_cos
            coarse_ref[at, ROWS : 2 * ROWS, :] = coarse_sin
            for a in range(TILE // ROWS):
                u_cos = coarse_ref[at, pl.ds(a, 1), :]
                u_sin = coarse_ref[at, pl.ds(ROWS + a, 1), :]
                rows = pl.ds(a * ROWS, ROWS)
                t_ref[g, i, rows, 0:LANE] = (u_cos * fine_cos - u_sin * fine_sin).astype(BF16)
                t_ref[g, i, rows, LANE : 2 * LANE] = (-(u_sin * fine_cos + u_cos * fine_sin)).astype(BF16)
        return carry

    lax.fori_loop(0, group, one, 0)


def phase_tables(local_pairs, m_lanes, chunks):
    pairs = local_pairs.shape[0]
    groups = m_lanes.shape[0]
    group = group_of(pairs)
    count = (4 * local_pairs + 20).astype(F32)
    specs, shapes = [], []
    for ng in chunks:
        specs.append(pl.BlockSpec((ng, group, TILE, 2 * LANE), lambda p, *_: (0, p, 0, 0)))
        specs.append(pl.BlockSpec((ng, group, 2 * ROWS, LANE), lambda p, *_: (0, p, 0, 0)))
        shapes.append(pltpu.HBM((ng, pairs, TILE, 2 * LANE), BF16))
        shapes.append(pltpu.HBM((ng, pairs, 2 * ROWS, LANE), F32))
    return pl.pallas_call(
        functools.partial(table_kernel, chunks),
        grid_spec=pltpu.PrefetchScalarGridSpec(
            num_scalar_prefetch=3,
            grid=(pairs // group,),
            in_specs=[pl.BlockSpec((groups, 1, LANE), lambda p, *_: (0, 0, 0))],
            out_specs=specs,
            scratch_shapes=[pltpu.VMEM((groups, 2 * ROWS, LANE), F32)],
        ),
        out_shape=shapes,
        compiler_params=params(48),
        cost_estimate=cost(10 * groups * pairs * TILE * 2 * LANE, 2 * groups * pairs * TILE * 2 * LANE),
        name="tables",
    )(count, 1.0 / count, 1.0 / jnp.sqrt(count), m_lanes)


def place_tiles(blocks, group, slot_ref, room_ref, x_ref, o_ref, s_ref):
    sources, share, fields, cap, width = x_ref.shape

    def unpack(source, carry):
        for l in range(share):
            for f in range(fields):
                value = x_ref[source, l, f].astype(F32)
                for h in range(2):
                    for t in range(TILE // LANE):
                        start = h * TILE + t * LANE
                        first = source * (cap * SPAN) + (h * 8 + f * share + l)
                        s_ref[t, pl.ds(first, cap, stride=SPAN), :] = value[:, start : start + LANE]
        return carry

    lax.fori_loop(0, sources, unpack, 0)
    lane = lax.broadcasted_iota(jnp.int32, (ROWS, LANE), 1)

    seen = 0
    for k, count in enumerate(blocks):

        def place(step, carry, seen=seen):
            for i in range(group):
                local = step * group + i
                first, room = slot_ref[seen + local] * SPAN, room_ref[seen + local]
                rows = pl.ds(pl.multiple_of((seen + local) * ROWS, ROWS), ROWS)
                for t in range(TILE // LANE):
                    value = s_ref[t, pl.ds(first, ROWS), :]
                    value = jnp.where(lane < room - t * LANE, value, 0.0)
                    o_ref[rows, t * LANE : (t + 1) * LANE] = value.astype(BF16)
            return carry

        lax.fori_loop(0, count, place, 0)
        seen += count * group


def rows_stage(blocks, lf, waves, pairs, stage, x_ref, t_ref, w_ref, o_ref, f_ref):
    many, group = t_ref.shape[:2]
    order = row_order(lf)
    cgs = -(-len(order) // waves)

    def pack(start, g, carry):
        for cg in range(cgs):
            items = []
            for p in range(cg * waves, (cg + 1) * waves):
                if p < len(order):
                    kind, row = order[p]
                    top = (kind * 2 * lf + row) * (group + 1)
                    items.append(f_ref[g, top : top + group, :])
                else:
                    items.append(jnp.zeros((group, LANE), F32))
            lane = pl.multiple_of((g * cgs + cg) * LANE, LANE)
            for d, value in enumerate(swap_blocks(items, LANE // waves)):
                top = d * pairs + start
                o_ref[top : top + group, pl.ds(lane, LANE)] = value.astype(BF16)
        return carry

    base = 0
    for k, count in enumerate(blocks):

        def bucket(base=base, count=count, k=k):
            def one(g, carry):
                for i in range(group):
                    rows = pl.ds((base + i * count) * ROWS, count * ROWS)
                    y = jnp.dot(x_ref[rows, :], t_ref[g, i], preferred_element_type=F32)
                    re = im = None
                    for b in range(count):
                        y_re = y[b * ROWS : (b + 1) * ROWS, 0:LANE]
                        y_im = y[b * ROWS : (b + 1) * ROWS, LANE : 2 * LANE]
                        w_cos = w_ref[g, i, b : b + 1, :]
                        w_sin = w_ref[g, i, ROWS + b : ROWS + b + 1, :]
                        add_re = w_cos * y_re + w_sin * y_im
                        add_im = w_cos * y_im - w_sin * y_re
                        re = add_re if re is None else re + add_re
                        im = add_im if im is None else im + add_im
                    for a, part in enumerate((re, im)):
                        part = part.astype(BF16).astype(F32)
                        north, south = part[0:8], part[8:16]
                        for s, total in enumerate((north + south, north - south)):
                            start = (s * 2 * lf + a * lf) * (group + 1) + i
                            f_ref[g, pl.ds(start, lf, stride=group + 1), :] = total[0:lf]
                return carry

            lax.fori_loop(0, many, one, 0)
            lax.fori_loop(0, many, functools.partial(pack, k * group), 0)

        pl.when(stage == k)(bucket)
        base += count * group

def rows_kernel(blocks, lf, waves, pairs, k_ref, t_ref, w_ref, o_ref, f_ref, x_ref, sems):
    step = pl.program_id(0)
    group = pairs // len(blocks)
    copies = []
    base = 0
    for k, count in enumerate(blocks):
        rows = pl.ds(base * ROWS, count * group * ROWS)
        copies.append(pltpu.make_async_copy(k_ref.at[rows], x_ref.at[rows], sems.at[k]))
        base += count * group

    def begin():
        for copy in copies:
            copy.start()

    pl.when(step == 0)(begin)
    for k, copy in enumerate(copies):
        pl.when(step == k)(copy.wait)
    rows_stage(blocks, lf, waves, pairs, step, x_ref, t_ref, w_ref, o_ref, f_ref)


def first_kernel(
    blocks, lf, waves, pairs, slot_ref, room_ref, a_ref, ahead_ref, t_ref, w_ref, o_ref, k_ref,
    f_ref, s_ref, x_ref, sem
):
    del ahead_ref
    step = pl.program_id(0)
    group = pairs // len(blocks)
    keep = pltpu.make_async_copy(x_ref, k_ref, sem)

    def begin():
        place_tiles(blocks, group, slot_ref, room_ref, a_ref, x_ref, s_ref)
        keep.start()

    pl.when(step == 0)(begin)
    rows_stage(blocks, lf, waves, pairs, step - 1, x_ref, t_ref, w_ref, o_ref, f_ref)
    pl.when(step == len(blocks))(keep.wait)


def table_specs(table, blocks, lag):
    ng, pairs, rows, lanes = table.shape
    at = lambda k, *_: (0, jnp.maximum(k - lag, 0), 0, 0)
    group = pairs // len(blocks)
    return [
        pl.BlockSpec((ng, group, rows, lanes), at),
        pl.BlockSpec((ng, group, 2 * ROWS, LANE), at),
    ]


def rows_cost(blocks, table, twist):
    ng, pairs, rows, lanes = table.shape
    taps = sum(blocks) * (pairs // len(blocks)) * ROWS * rows
    return cost(ng * 2 * taps * lanes, 2 * taps + 2 * table.size + 4 * twist.size)


def first_rows(arrived, slots, room, ahead, table, twist, blocks, lf, waves):
    sources, share, fields, cap, width = arrived.shape
    ng, pairs = table.shape[:2]
    cgs = -(-4 * lf // waves)
    return pl.pallas_call(
        functools.partial(first_kernel, blocks, lf, waves, pairs),
        grid_spec=pltpu.PrefetchScalarGridSpec(
            num_scalar_prefetch=2,
            grid=(len(blocks) + 1,),
            in_specs=[
                pl.BlockSpec(memory_space=pltpu.VMEM),
                pl.BlockSpec(memory_space=pl.ANY),
            ]
            + table_specs(table, blocks, 1),
            out_specs=[
                pl.BlockSpec((waves * pairs, ng * cgs * LANE), lambda k, *_: (0, 0)),
                pl.BlockSpec(memory_space=pl.ANY),
            ],
            scratch_shapes=[
                pltpu.VMEM((ng, 4 * lf * (pairs // len(blocks) + 1), LANE), F32),
                pltpu.VMEM((TILE // LANE, sources * cap * SPAN, LANE), F32),
                pltpu.VMEM((slots.shape[0] * ROWS, TILE), BF16),
                pltpu.SemaphoreType.DMA,
            ],
        ),
        out_shape=[
            pltpu.HBM((waves * pairs, ng * cgs * LANE), BF16),
            pltpu.HBM((slots.shape[0] * ROWS, TILE), BF16),
        ],
        compiler_params=params(48),
        cost_estimate=rows_cost(blocks, table, twist),
        name="place_and_rows",
    )(slots, room, arrived, ahead, table, twist)


def rows_to_waves(tiles, table, twist, blocks, lf, waves):
    ng, pairs = table.shape[:2]
    cgs = -(-4 * lf // waves)
    return pl.pallas_call(
        functools.partial(rows_kernel, blocks, lf, waves, pairs),
        grid=(len(blocks),),
        in_specs=[pl.BlockSpec(memory_space=pl.ANY)]
        + table_specs(table, blocks, 0),
        out_specs=pl.BlockSpec((waves * pairs, ng * cgs * LANE), lambda k: (0, 0)),
        out_shape=pltpu.HBM((waves * pairs, ng * cgs * LANE), BF16),
        scratch_shapes=[
            pltpu.VMEM((ng, 4 * lf * (pairs // len(blocks) + 1), LANE), F32),
            pltpu.VMEM(tiles.shape, BF16),
            pltpu.SemaphoreType.DMA((len(blocks),)),
        ],
        compiler_params=params(60),
        cost_estimate=rows_cost(blocks, table, twist),
        name="rows_to_waves",
    )(tiles, table, twist)


def legendre_kernel(g0, per_group, waves, lf, total, own_ref, r_ref, p_ref, l_ref, *rest):
    s_ref, o_ref, d_ref, b_ref = rest[-4:]
    width = LANE // waves
    span = width + 1
    group, stage = pl.program_id(0), pl.program_id(1)
    many = l_ref.shape[0]
    order = row_order(lf)
    tiles = len(order) // 8
    rows = r_ref.shape[1]
    coefs = l_ref.shape[1]
    lanes = l_ref.shape[2] // LANE

    def begin():
        value = lax.dot_general(
            r_ref[...], p_ref[...], (((0,), (0,)), ((), ())), preferred_element_type=F32
        )
        for p in range(rows // width):
            for t in range(lanes):
                d_ref[t, p * span : p * span + width, :] = value[
                    p * width : (p + 1) * width, t * LANE : (t + 1) * LANE
                ]
        if rows > len(order) * width:
            b_ref[...] = jnp.zeros_like(b_ref)

    pl.when(stage == 0)(begin)
    ordinal = lax.broadcasted_iota(jnp.int32, (8, coefs), 1)
    low_rows = lax.broadcasted_iota(jnp.int32, (8, coefs), 0) < 4

    for i in range(many):
        local = stage * many + i
        q = own_ref[(g0 + group) * per_group + local]

        def where_rows(w, tile, local=local):
            return pl.ds(tile * 8 * span + 2 * local + w, 8, stride=span)

        picked = []
        for w in range(2):
            for tile in range(tiles):
                cut = where_rows(w, tile)
                picked.append(jnp.concatenate([d_ref[t, cut, :] for t in range(lanes)], axis=1))
        left = jnp.concatenate(picked, axis=0).astype(BF16)
        forward = lax.dot_general(
            left, l_ref[i], (((1,), (1,)), ((), ())), preferred_element_type=F32
        )
        split = total - q
        low = ordinal < split
        even = jnp.where(low, ordinal & 1, (ordinal - split) & 1) == 0
        chosen = [
            jnp.where(low, forward[t * 8 : t * 8 + 8], forward[(tiles + t) * 8 : (tiles + t) * 8 + 8])
            for t in range(tiles)
        ]
        head = jnp.where(even, chosen[0], chosen[1])
        tail = jnp.where(even, chosen[2], pltpu.roll(chosen[2], 4, 0))
        s_ref[i, 0:8, :] = head
        s_ref[i, 8:12, :] = tail[0:4]
        degree = jnp.where(low, q + ordinal, ordinal - 1).astype(F32)
        damping = 1.0 / (1.0 + 8.0 * degree * (degree + 1.0) / (total * total))
        head = head * damping
        tail = tail * damping
        tail = jnp.where(low_rows, tail, pltpu.roll(tail, 4, 0))
        parts = [head, jnp.where(even, head, -head), jnp.where(even | low_rows, tail, -tail)]
        back = jnp.concatenate(
            [jnp.where(low, x, 0.0) for x in parts] + [jnp.where(low, 0.0, x) for x in parts], axis=0
        ).astype(BF16)
        rebuilt = jnp.dot(back, l_ref[i], preferred_element_type=F32)
        for w in range(2):
            for tile in range(tiles):
                row = (w * tiles + tile) * 8
                cut = where_rows(w, tile)
                for t in range(lanes):
                    b_ref[t, cut, :] = rebuilt[row : row + 8, t * LANE : (t + 1) * LANE]

    def end():
        lines = []
        for p in range(rows // width):
            cut = pl.ds(p * span, width)
            lines.append(jnp.concatenate([b_ref[t, cut, :] for t in range(lanes)], axis=1))
        value = jnp.concatenate(lines, axis=0).astype(BF16)
        o_ref[...] = lax.dot_general(
            p_ref[...], value, (((1,), (1,)), ((), ())), preferred_element_type=F32
        ).astype(BF16)

    pl.when(stage == pl.num_programs(1) - 1)(end)


def legendre_both(received, places, legendre, own_sets, lf, waves, chunk, spectral):
    sets, coefs, pair_total = legendre.shape
    cgs = -(-4 * lf // waves)
    rows = cgs * LANE
    per_group = LANE // waves // 2
    many = min(8, per_group)
    stages = per_group // many
    g0, ng = chunk
    block = lambda g, k, *_: ((g0 + g) * stages + k, 0, 0)
    in_specs = [
        pl.BlockSpec((pair_total, rows), lambda g, k, *_: (0, g)),
        pl.BlockSpec((pair_total, pair_total), lambda g, k, *_: (0, 0)),
        pl.BlockSpec((many, coefs, pair_total), block),
    ]
    operands = [own_sets, received, places, legendre]
    aliases = {}
    if spectral is not None:
        in_specs.append(pl.BlockSpec(memory_space=pl.ANY))
        operands.append(spectral)
        aliases = {4: 0}
    return pl.pallas_call(
        functools.partial(legendre_kernel, g0, per_group, waves, lf, coefs - 1),
        grid_spec=pltpu.PrefetchScalarGridSpec(
            num_scalar_prefetch=1,
            grid=(ng, stages),
            in_specs=in_specs,
            out_specs=[
                pl.BlockSpec((many, 2 * lf, coefs), block),
                pl.BlockSpec((pair_total, rows), lambda g, k, *_: (0, g)),
            ],
            scratch_shapes=[
                pltpu.VMEM((pair_total // LANE, cgs * (LANE + waves), LANE), F32),
                pltpu.VMEM((pair_total // LANE, cgs * (LANE + waves), LANE), F32),
            ],
        ),
        out_shape=[
            jax.ShapeDtypeStruct((sets, 2 * lf, coefs), F32),
            pltpu.HBM((pair_total, ng * rows), BF16),
        ],
        input_output_aliases=aliases,
        compiler_params=params(60),
        cost_estimate=cost(
            ng * per_group * 4 * 48 * coefs * pair_total, ng * per_group * 2 * coefs * pair_total
        ),
        name="legendre",
    )(*operands)


def unpack_kernel(order, lf, *refs):
    perm_ref, o_ref, g_ref = refs[-3:]
    parts = refs[:-3]
    sources, piece = parts[0].shape[0], parts[0].shape[1]
    cgs = -(-len(order) // sources)
    g = 0
    for ref in parts:
        for local in range(ref.shape[2] // (cgs * LANE)):
            for cg in range(cgs):
                start = (local * cgs + cg) * LANE
                items = [ref[s, :, start : start + LANE] for s in range(sources)]
                for d, value in enumerate(swap_blocks(items, LANE // sources)):
                    p = cg * sources + d
                    if p < len(order):
                        kind, row = order[p]
                        top = (kind * 2 * lf + row) * piece
                        g_ref[g, top : top + piece, :] = value
            g += 1
    left = jnp.concatenate([g_ref[t] for t in range(g)], axis=1)
    value = jnp.dot(left, perm_ref[...], preferred_element_type=F32).astype(BF16)
    o_ref[...] = value.reshape(o_ref.shape)


def unpack_rows(parts, perm, lf, waves):
    pairs = parts[0].shape[0] // waves
    piece = 16 if pairs % 16 == 0 else pairs
    total = perm.shape[0]
    shaped = [x.reshape(waves, pairs, x.shape[1]) for x in parts]
    size = sum(x.size for x in shaped)
    return pl.pallas_call(
        functools.partial(unpack_kernel, row_order(lf), lf),
        grid=(pairs // piece,),
        in_specs=[pl.BlockSpec((waves, piece, x.shape[2]), lambda j: (0, j, 0)) for x in shaped]
        + [
            pl.BlockSpec((total, total), lambda j: (0, 0)),
        ],
        out_specs=pl.BlockSpec((4 * lf, piece, total), lambda j: (0, j, 0)),
        out_shape=jax.ShapeDtypeStruct((4 * lf, pairs, total), BF16),
        scratch_shapes=[pltpu.VMEM((total // LANE, piece * 4 * lf, LANE), BF16)],
        compiler_params=params(32),
        cost_estimate=cost(2 * size * total, 4 * size),
        name="unpack",
    )(*shaped, perm)


def body(grid_fields, diffusivity, tile_map, pair_order, m_order, legendre):
    waves = lax.axis_size("wave")
    groups = lax.axis_size("lev")
    me = lax.axis_index("wave")
    levels, fields, slots, width = grid_fields.shape
    cap = slots // waves
    share = levels // groups
    lf = share * fields
    pair_total = pair_order.shape[0]
    pairs = pair_total // waves
    set_total = m_order.shape[0]
    sets = set_total // waves
    waves_total = 2 * set_total
    lane_groups = waves_total // LANE
    run = LANE // waves

    outgoing = diffuse(grid_fields, diffusivity, waves, groups)
    outgoing = outgoing.reshape(waves * groups, share, fields, cap, width)
    arrived = lax.all_to_all(outgoing, ("wave", "lev"), 0, 0, tiled=True)

    local_pairs = lax.dynamic_slice_in_dim(pair_order, me * pairs, pairs)
    picks = jnp.stack([m_order, waves_total - 1 - m_order], axis=1)
    m_lanes = picks.reshape(waves, lane_groups, run).transpose(1, 0, 2)
    m_lanes = m_lanes.reshape(lane_groups, 1, LANE).astype(F32)
    chunks = CHUNKS if sum(CHUNKS) == lane_groups else (lane_groups,)
    tables = phase_tables(local_pairs, m_lanes, chunks)

    group = group_of(pairs)
    stages = pairs // group
    blocks = []
    for k in range(stages):
        largest = waves * (k * group + group - 1) + waves - 1
        blocks.append(min(BLK, -(-(4 * largest + 20) // TILE)))
    pair_at = [k * group + i for k in range(stages) for i in range(group) for _ in range(blocks[k])]
    block_at = [b for k in range(stages) for i in range(group) for b in range(blocks[k])]
    pair_at = jnp.asarray(pair_at, jnp.int32)
    block_at = jnp.asarray(block_at, jnp.int32)
    pair_ids = jnp.take(local_pairs, pair_at)
    wanted = pair_ids * BLK + block_at
    room = 4 * pair_ids + 20 - block_at * TILE
    catalog = tile_map.reshape(waves, groups, waves, cap)
    own = lax.dynamic_index_in_dim(catalog, me, axis=2, keepdims=False).reshape(-1)
    slot_ids = jnp.arange(own.shape[0], dtype=jnp.int32)
    found = jnp.where(own[None, :] == wanted[:, None], slot_ids[None, :], 0)
    slot_of = jnp.max(found, axis=1)

    places = (pair_order[:, None] == jnp.arange(pair_total, dtype=jnp.int32)[None, :]).astype(BF16)
    own_sets = lax.dynamic_slice_in_dim(m_order, me * sets, sets)
    lane = jnp.arange(waves_total, dtype=jnp.int32)
    spot = lane // LANE * run + lane % run
    column = spot % 2 * set_total + lane % LANE // run * sets + spot // 2
    perm = (column[:, None] == lane[None, :]).astype(BF16)

    received = []
    for c in range(len(chunks)):
        pieces = tables[2 * c], tables[2 * c + 1], tuple(blocks), lf, waves
        if c == 0:
            sent, tiles = first_rows(arrived, slot_of, room, legendre, *pieces)
        else:
            sent = rows_to_waves(tiles, *pieces)
        received.append(lax.all_to_all(sent, "wave", 0, 0, tiled=True))
    spectral = None
    returned = []
    begin = 0
    for ng, part in zip(chunks, received):
        spectral, back = legendre_both(
            part, places, legendre, own_sets, lf, waves, (begin, ng), spectral
        )
        begin += ng
        returned.append(lax.all_to_all(back, "wave", 0, 0, tiled=True))
    fourier_out = unpack_rows(returned, perm, lf, waves)
    spectral = spectral.reshape(sets, 2, fields, share, legendre.shape[1])
    fourier_out = fourier_out.transpose(1, 0, 2).reshape(pairs, 2, 2, fields, share, waves_total)
    return spectral, fourier_out


def solution(mesh):
    return jax.shard_map(
        body,
        mesh=mesh,
        in_specs=(
            P(None, None, ("wave", "lev"), None),
            P(None, ("wave", "lev"), None),
            P(),
            P(),
            P(),
            P("wave", None, None),
        ),
        out_specs=(P("wave", None, None, "lev", None), P("wave", None, None, None, "lev", None)),
        check_vma=False,
    )
```
